32 devices in a mesh: gen: 8 (over z, x), tm: 4 (over y, core).
Axes of the slice: x: 2, y: 2, z: 4, core: 2. Of those that a mesh axis runs over, the one named last changes fastest.
Arguments:
- relation: bfloat16 [6400, 6400], P('gen', 'tm'), may hold values from -1 to 3
- effects: float32 [6400, 1024], P('tm', 'gen'), may hold values from -6 to 6
- phi_one: float32 [1024], replicated, may hold values from 0.3 to 1.2
- phi_two: float32 [1024], replicated, may hold values from -0.7 to 0.3
- innov_scale: float32 [1024], replicated, may hold values from 0.4 to 2.5
Outputs:
- applied: float32 [6400, 1024], P('gen', 'tm')
The draws below stay inside these ranges and needn't reach their ends.
All inputs are finite; a program needn't handle non-finite values.
Results may differ from the reference program's by a relative error of at most 0.0003.
Values sent between devices are 32-bit elements; how exact they have to be, the bound alone decides.
No kernel may reach another device: no remote copies, remote signals or barrier semaphores. Data moves between devices by JAX's collectives and lax.ppermute only.
A program may use at most 64 MiB of HBM per device.

```python
import math
import jax
import jax.numpy as jnp
from jax import lax

ANI_DEV = 800
TIMES = 1024
ANIMALS = 6400
N_GEN = 8


def draw_relation(key, part):
    key_off, key_diag = jax.random.split(jax.random.fold_in(key, 11))
    spread = ANIMALS ** (-0.5)
    raw = jnp.clip(jax.random.normal(key_off, (ANIMALS, ANIMALS), jnp.float32), -6.0, 6.0)
    indices = jnp.arange(ANIMALS, dtype=jnp.int32)
    upper = indices[:, None] < indices[None, :]
    offdiag = jnp.where(upper, raw, raw.T) * spread
    diagonal = jax.random.uniform(key_diag, (ANIMALS,), jnp.float32, 1.5, 2.5)
    on_diag = indices[:, None] == indices[None, :]
    return jnp.where(on_diag, diagonal[None, :], offdiag).astype(jnp.bfloat16)


def block_scale(stream_key, dims, shards, smallest, high):
    def one(dim, shards_of):
        steps = jax.random.uniform(jax.random.fold_in(jax.random.fold_in(stream_key, 6), dim), (shards_of,), jnp.float32, smallest / len(shards), high / len(shards))
        return jnp.repeat(jnp.exp(steps), dims[dim] // shards_of).reshape((-1,) + (1,) * (len(dims) - dim - 1))

    gain = one(*shards[0])
    for cut in shards[1:]:
        gain = gain * one(*cut)
    return gain


def normal_values(key, dims, width, most, shards=(), kind=jnp.bfloat16):
    values = jax.random.normal(key, dims, jnp.float32) * width
    if len(shards) > 0:
        values = block_scale(key, dims, shards, -0.22, 0.18) * values
    return jnp.clip(values, min=-most, max=most).astype(kind)


def setup_inputs(seed: int = 0) -> dict:
    keys = jax.random.split(jax.random.key(seed), 6)
    relation = draw_relation(jax.random.fold_in(keys[5], 71), 0)
    effects = normal_values(keys[1], (ANIMALS, TIMES), 1.0, 6.0, ((0, 4), (1, 8)), jnp.float32)
    phi_one = jnp.clip(jax.random.uniform(keys[2], (TIMES,), jnp.float32, 0.3, 1.2), 0.3, 1.2)
    phi_two = jnp.clip(jax.random.uniform(keys[3], (TIMES,), jnp.float32, -0.7, 0.3), -0.7, 0.3)
    innov_scale = jnp.clip(jnp.exp(jax.random.uniform(keys[4], (TIMES,), jnp.float32, math.log(0.4), math.log(2.5))), 0.4, 2.5)
    return dict(relation=relation, effects=effects, phi_one=phi_one, phi_two=phi_two, innov_scale=innov_scale)


def temporal_apply(field, phi_one, phi_two, innov_scale):
    zero_pair = jnp.zeros((2,), jnp.float32)
    first_pad = jnp.concatenate([phi_one, zero_pair])
    second_pad = jnp.concatenate([phi_two, zero_pair])
    scale_pad = jnp.concatenate([innov_scale, zero_pair])
    widened = jnp.pad(field, ((0, 0), (2, 2)))
    innov = widened[:, 2:] - first_pad[None, :] * widened[:, 1:-1] - second_pad[None, :] * widened[:, :-2]
    weighted = scale_pad[None, :] * innov
    count = field.shape[1]
    return (weighted[:, :count]
            - first_pad[None, 1:count + 1] * weighted[:, 1:count + 1]
            - second_pad[None, 2:count + 2] * weighted[:, 2:count + 2])


def reference(relation, effects, phi_one, phi_two, innov_scale):
    row_blocks = relation.reshape(N_GEN, ANI_DEV, ANIMALS)

    def block_rows(rows):
        return jnp.dot(rows.astype(jnp.float32), effects, precision=lax.Precision.HIGHEST,
                       preferred_element_type=jnp.float32)

    genetic = lax.map(block_rows, row_blocks).reshape(ANIMALS, TIMES)
    return temporal_apply(genetic, phi_one, phi_two, innov_scale)
```

```python
import jax
import jax.numpy as jnp
from jax import lax
from jax.experimental import pallas as pl
from jax.experimental.pallas import tpu as pltpu
from jax.sharding import PartitionSpec as P

VMEM_LIMIT = 40 * 1024 * 1024


def bands(phi_one, phi_two, innov_scale):
    zero_pair = jnp.zeros((2,), jnp.float32)
    first = jnp.concatenate([phi_one, zero_pair])
    second = jnp.concatenate([phi_two, zero_pair])
    scale = jnp.concatenate([innov_scale, zero_pair])
    count = phi_one.shape[0]
    first_0, first_1, first_2 = first[:count], first[1 : count + 1], first[2:]
    second_0, second_1, second_2 = second[:count], second[1 : count + 1], second[2:]
    scale_0, scale_1, scale_2 = scale[:count], scale[1 : count + 1], scale[2:]
    return jnp.stack(
        [
            -scale_0 * second_0,
            first_1 * scale_1 * second_1 - scale_0 * first_0,
            scale_0 + first_1 * first_1 * scale_1 + second_2 * second_2 * scale_2,
            second_2 * scale_2 * first_2 - first_1 * scale_1,
            -second_2 * scale_2,
        ]
    )


def edge(cells, pairs):
    flat = lax.ppermute(cells.T.reshape(-1), "gen", pairs)
    return flat.reshape(2, cells.shape[0]).T


def banded(effects, weights):
    gens = lax.axis_size("gen")
    rows, width = effects.shape
    before = edge(effects[:, width - 2 :], [(i, i + 1) for i in range(gens - 1)])
    after = edge(effects[:, :2], [(i + 1, i) for i in range(gens - 1)])
    start = lax.axis_index("gen") * width
    mine = lax.dynamic_slice_in_dim(weights, start, width, axis=1)
    widened = jnp.concatenate([before, effects, after], axis=1)
    return sum(mine[j][None, :] * widened[:, j : j + width] for j in range(5))


def product_of(relation_ref, halves):
    block = jnp.concatenate([half[...] for half in halves], axis=0)
    high = block.astype(jnp.bfloat16)
    low = (block - high.astype(jnp.float32)).astype(jnp.bfloat16)
    both = jnp.dot(
        relation_ref[...],
        jnp.concatenate([high, low], axis=1),
        preferred_element_type=jnp.float32,
    )
    width = block.shape[1]
    return both[:, :width] + both[:, width:]


def one_kernel(relation_ref, top_ref, bottom_ref, out_ref):
    out_ref[...] = product_of(relation_ref, (top_ref, bottom_ref))


def pair_kernel(flag_ref, relation_ref, top_ref, bottom_ref, other_ref, send_ref, keep_ref):
    made = product_of(relation_ref, (top_ref, bottom_ref))
    other = other_ref[...]
    keep_other = flag_ref[0] == 1
    send_ref[...] = jnp.where(keep_other, made, other)
    keep_ref[...] = jnp.where(keep_other, other, made)


def call(kernel, outs, relation, operands, scalars=()):
    rows, depth = relation.shape
    width = operands[0].shape[1]
    whole = pl.BlockSpec(memory_space=pltpu.VMEM)
    return pl.pallas_call(
        kernel,
        out_shape=[jax.ShapeDtypeStruct((rows, width), jnp.float32)] * outs,
        in_specs=[pl.BlockSpec(memory_space=pltpu.SMEM)] * len(scalars)
        + [whole] * (1 + len(operands)),
        out_specs=[whole] * outs,
        compiler_params=pltpu.CompilerParams(vmem_limit_bytes=VMEM_LIMIT),
        cost_estimate=pl.CostEstimate(
            flops=4 * rows * depth * width, bytes_accessed=4 * rows * width, transcendentals=0
        ),
    )(*scalars, relation, *operands)


def ring_plan(gens, tms):
    order = list(range(0, gens, 2)) + list(range(gens - 1, 0, -2))
    place = {g: p for p, g in enumerate(order)}
    share = gens // tms
    return order, place, share


def by_ring(relation, effects, phi_one, phi_two, innov_scale):
    gens, tms = lax.axis_size("gen"), lax.axis_size("tm")
    order, place, share = ring_plan(gens, tms)
    half = gens // 2
    forward = [(order[p], order[(p + 1) % gens]) for p in range(gens)]
    backward = [(b, a) for a, b in forward]
    swap = [(t, t ^ 1) for t in range(tms)]

    gen, tm = lax.axis_index("gen"), lax.axis_index("tm")
    own = banded(effects, bands(phi_one, phi_two, innov_scale))
    depth = own.shape[0]
    cut = depth // 256 * 128
    top, bottom = own[:cut], own[cut:]

    blocks = {0: (top, bottom)}
    for step in range(1, half):
        behind, ahead = blocks[1 - step], blocks[step - 1]
        behind_top = lax.ppermute(behind[0], "gen", forward)
        ahead_bottom = lax.ppermute(ahead[1], "gen", backward)
        behind_bottom = lax.ppermute(behind[1], "gen", forward)
        ahead_top = lax.ppermute(ahead[0], "gen", backward)
        blocks[-step] = (behind_top, behind_bottom)
        blocks[step] = (ahead_top, ahead_bottom)
    last = half - 1
    blocks[-half] = (
        lax.ppermute(blocks[-last][0], "gen", forward),
        lax.ppermute(blocks[last][1], "gen", backward),
    )

    products = {}
    for far in [0] + [s for n in range(1, half // 2 + 1) for s in (n, -n)]:
        if far != -(half // 2):
            products[far] = call(one_kernel, 1, relation, blocks[far])[0]

    first_block = {}
    summed = {}
    for near, far in ((2, -2), (1, -3), (-1, 3), (0, -4)):
        owner = {
            d: [order[(place[g] + d) % gens] // share for g in range(gens)] for d in (near, far)
        }
        keep_near = (jnp.asarray([t % 2 for t in owner[near]])[gen] == tm % 2).astype(jnp.int32)
        send, keep = call(
            pair_kernel, 2, relation, (*blocks[far], products[near]), (keep_near.reshape(1),)
        )
        chip_sum = keep + lax.ppermute(send, "tm", swap)
        across = [
            (g * tms + (t ^ 2), g * tms + t)
            for d in (near, far)
            for g, t in enumerate(owner[d])
        ]
        total = chip_sum + lax.ppermute(chip_sum, ("gen", "tm"), across)
        for d in (near, far):
            for j in range(share):
                holds = jnp.asarray(
                    [order[(place[g] + d) % gens] % share == j for g in range(gens)]
                )[gen]
                mine = holds & (jnp.asarray(owner[d])[gen] == tm)
                summed.setdefault(j, []).append((mine, total))
        first_block[near] = keep_near
    columns = []
    for j in range(share):
        column = summed[j][0][1]
        for mine, total in summed[j][1:]:
            column = jnp.where(mine, total, column)
        columns.append(column)
    return jnp.concatenate(columns, axis=1)


def extended(cells, sides, width):
    for axis, dim in sides:
        count = lax.axis_size(axis)
        ends = count - 1
        head = lax.slice_in_dim(cells, 0, width, axis=dim)
        tail = lax.slice_in_dim(cells, cells.shape[dim] - width, cells.shape[dim], axis=dim)
        cells = jnp.concatenate(
            [
                lax.ppermute(tail, axis, [(i, (i + 1) % count) for i in range(ends)]),
                cells,
                lax.ppermute(head, axis, [((i + 1) % count, i) for i in range(ends)]),
            ],
            axis=dim,
        )
    return cells


def temporal_block(widened, first_time, phi_one, phi_two, innov_scale):
    block = widened.shape[1] - 4
    zero_pair = jnp.zeros((2,), jnp.float32)
    first_pad = jnp.concatenate([phi_one, zero_pair])
    second_pad = jnp.concatenate([phi_two, zero_pair])
    scale_pad = jnp.concatenate([innov_scale, zero_pair])
    first_win = lax.dynamic_slice_in_dim(first_pad, first_time, block + 2)
    second_win = lax.dynamic_slice_in_dim(second_pad, first_time, block + 2)
    scale_win = lax.dynamic_slice_in_dim(scale_pad, first_time, block + 2)
    innov = (
        widened[:, 2:]
        - first_win[None, :] * widened[:, 1:-1]
        - second_win[None, :] * widened[:, :-2]
    )
    weighted = scale_win[None, :] * innov
    first_next = lax.dynamic_slice_in_dim(first_pad, first_time + 1, block)
    second_next = lax.dynamic_slice_in_dim(second_pad, first_time + 2, block)
    return (
        weighted[:, :block]
        - first_next[None, :] * weighted[:, 1 : block + 1]
        - second_next[None, :] * weighted[:, 2 : block + 2]
    )


def by_gather(relation, effects, phi_one, phi_two, innov_scale):
    relation_wide = relation.astype(jnp.float32)
    partial_sums = jnp.dot(
        relation_wide,
        lax.all_gather(effects, "gen", axis=1, tiled=True),
        precision=lax.Precision.HIGHEST,
        preferred_element_type=jnp.float32,
    )
    genetic = lax.psum_scatter(partial_sums, "tm", scatter_dimension=1, tiled=True)
    widened_time = extended(genetic, (("tm", 1),), 2)
    start_tm = lax.axis_index("tm") * genetic.shape[1]
    return temporal_block(widened_time, start_tm, phi_one, phi_two, innov_scale)


def on_device(relation, effects, phi_one, phi_two, innov_scale):
    gens, tms = lax.axis_size("gen"), lax.axis_size("tm")
    fits = gens == 8 and tms == 4 and effects.shape[1] % 128 == 0 and effects.shape[0] % 8 == 0
    way = by_ring if fits else by_gather
    return way(relation, effects, phi_one, phi_two, innov_scale)


def solution(mesh):
    placed = (P("gen", "tm"), P("tm", "gen"), P(), P(), P())
    return jax.shard_map(
        on_device, mesh=mesh, in_specs=placed, out_specs=P("gen", "tm"), check_vma=False
    )
```

```python
import jax
import jax.numpy as jnp
from jax import lax
from jax.experimental import pallas as pl
from jax.experimental.pallas import tpu as pltpu
from jax.sharding import PartitionSpec as P

VMEM_LIMIT = 12 * 1024 * 1024
WIDTH = 128
CORE_PIECES = 2
LAST_COST = 1
KERNEL_FLOPS = 10**8

WHOLE = pl.BlockSpec(memory_space=pltpu.VMEM)
SCALAR = pl.BlockSpec(memory_space=pltpu.SMEM)
ANYWHERE = pl.BlockSpec(memory_space=pl.ANY)


def call(kernel, shapes, operands, scratch=(), scalars=(), places=None, into=WHOLE, flops=0):
    return pl.pallas_call(
        kernel,
        out_shape=[jax.ShapeDtypeStruct(shape, jnp.float32) for shape in shapes],
        in_specs=[SCALAR] * len(scalars) + (places or [WHOLE] * len(operands)),
        out_specs=[into] * len(shapes),
        scratch_shapes=scratch,
        compiler_params=pltpu.CompilerParams(vmem_limit_bytes=VMEM_LIMIT),
        cost_estimate=pl.CostEstimate(flops=flops, bytes_accessed=0, transcendentals=0),
    )(*scalars, *operands)


def bands(phi_one, phi_two, innov_scale):
    count = phi_one.shape[1]
    row = lax.broadcasted_iota(jnp.int32, (8, count), 0)
    lane = lax.broadcasted_iota(jnp.int32, (8, count), 1)

    def rows(*values):
        out = jnp.zeros((8, count), jnp.float32)
        for n, value in enumerate(values):
            out = jnp.where(row == n, value, out)
        return out

    now = rows(phi_one, phi_two, innov_scale)
    next_1 = jnp.where(lane < count - 1, pltpu.roll(now, count - 1, 1), 0.0)
    next_2 = jnp.where(lane < count - 2, pltpu.roll(now, count - 2, 1), 0.0)
    first_0, second_0, scale_0 = (now[n : n + 1] for n in range(3))
    first_1, second_1, scale_1 = (next_1[n : n + 1] for n in range(3))
    first_2, second_2, scale_2 = (next_2[n : n + 1] for n in range(3))
    return rows(
        -scale_0 * second_0,
        first_1 * scale_1 * second_1 - scale_0 * first_0,
        scale_0 + first_1 * first_1 * scale_1 + second_2 * second_2 * scale_2,
        second_2 * scale_2 * first_2 - first_1 * scale_1,
        -second_2 * scale_2,
    )


def weights_kernel(one_ref, two_ref, scale_ref, weights_ref):
    weights_ref[...] = bands(one_ref[...][None], two_ref[...][None], scale_ref[...][None])


def products_kernel(relation_ref, *refs):
    both_ref, padded_ref = refs[-2:]
    count = (len(refs) - 2) // 4
    rows = relation_ref.shape[0]
    padded_ref[rows:] = jnp.zeros((padded_ref.shape[0] - rows, WIDTH), jnp.float32)
    for n in range(count):
        block = jnp.concatenate([refs[2 * n][...], refs[2 * n + 1][...]], axis=0)
        high = block.astype(jnp.bfloat16)
        low = (block - high.astype(jnp.float32)).astype(jnp.bfloat16)
        both_ref[...] = jnp.dot(
            relation_ref[...],
            jnp.concatenate([high, low], axis=1),
            preferred_element_type=jnp.float32,
        )
        made = both_ref[:, :WIDTH] + both_ref[:, WIDTH:]
        refs[2 * count + 2 * n][...] = made
        padded_ref[:rows] = made
        turned = padded_ref[...].T
        edges_ref = refs[2 * count + 2 * n + 1]
        edges_ref[0:2] = turned[0:2]
        edges_ref[2:4] = turned[WIDTH - 2 :]


def pairs_kernel(flag_ref, *refs):
    send_ref, keep_ref = refs[-2:]
    rows = refs[0].shape[0]
    for n in range((len(refs) - 2) // 2):
        here = pl.ds(n * rows, rows)
        for near in range(2):

            @pl.when(flag_ref[n] == near)
            def _():
                send_ref[here] = refs[2 * n + near][...]
                keep_ref[here] = refs[2 * n + 1 - near][...]


def borders_kernel(flag_ref, *refs):
    send_ref, keep_ref, edges_ref = refs[-3:]
    count = len(refs) - 3
    for n in range(count):
        edges_ref[n] = refs[n][...]
    edges_ref[count] = jnp.zeros_like(refs[0])
    for out_ref, first in ((send_ref, 0), (keep_ref, 2)):
        for n in range(2):
            before, after = flag_ref[2 * (first + n)], flag_ref[2 * (first + n) + 1]
            out_ref[4 * n : 4 * n + 2] = edges_ref[before][2:4]
            out_ref[4 * n + 2 : 4 * n + 4] = edges_ref[after][0:2]


def part_sums_kernel(flag_ref, keep_ref, *refs):
    send_ref, mine_ref = refs[-2:]
    rows = mine_ref.shape[0]
    pieces = (len(refs) - 2) // 2
    piece = rows // pieces
    for n in range(2):

        @pl.when(flag_ref[0] == n)
        def _():
            for sums_ref, first in ((mine_ref, n), (send_ref, 1 - n)):
                for m in range(pieces):
                    here = pl.ds(m * piece, piece)
                    there = pl.ds(first * rows + m * piece, piece)
                    sums_ref[here] = keep_ref[there] + refs[first * pieces + m][...]


def border_sums_kernel(flag_ref, keep_ref, got_ref, send_ref, mine_ref):
    rows = mine_ref.shape[0]
    for n in range(2):

        @pl.when(flag_ref[0] == n)
        def _():
            for sums_ref, first in ((mine_ref, n), (send_ref, 1 - n)):
                here = slice(first * rows, first * rows + rows)
                sums_ref[...] = keep_ref[here] + got_ref[here]


def last_kernel(
    flag_ref,
    odd_any,
    odd_got_any,
    two_any,
    two_got_any,
    zero_ref,
    zero_got_ref,
    mine_ref,
    got_ref,
    weights_ref,
    out_any,
    sums_ref,
    sides_ref,
    out_ref,
    sems,
    out_sems,
):
    odd, is_two = flag_ref[0], flag_ref[1]
    rows = out_any.shape[0]
    span = sides_ref.shape[1]
    copies = [
        pltpu.make_async_copy(odd_any, sums_ref.at[0], sems.at[0]),
        pltpu.make_async_copy(odd_got_any, sums_ref.at[1], sems.at[1]),
    ]
    two_copies = [
        pltpu.make_async_copy(two_any, sums_ref.at[2], sems.at[2]),
        pltpu.make_async_copy(two_got_any, sums_ref.at[3], sems.at[3]),
    ]
    for copy in copies:
        copy.start()

    @pl.when(is_two == 1)
    def _():
        for copy in two_copies:
            copy.start()

    start = pl.multiple_of(flag_ref[2] * (2 * WIDTH), 2 * WIDTH)
    weights = weights_ref[:, pl.ds(start, 2 * WIDTH)]
    row = lax.broadcasted_iota(jnp.int32, (8, span), 0)
    nothing = jnp.zeros((WIDTH - 8, span), jnp.float32)
    border = mine_ref[...] + got_ref[...]
    end = 2 * WIDTH - 1
    first = weights[0:1, 0:1] * border[0:1] + weights[1:2, 0:1] * border[1:2]
    second = weights[0:1, 1:2] * border[1:2]
    above = jnp.where(row == 0, first, jnp.where(row == 1, second, 0.0))
    last = weights[3:4, end:] * border[2:3] + weights[4:5, end:] * border[3:4]
    but_last = weights[4:5, end - 1 : end] * border[2:3]
    below = jnp.where(row == 7, last, jnp.where(row == 6, but_last, 0.0))
    sides_ref[0] = jnp.concatenate([above, nothing], axis=0).T
    sides_ref[1] = jnp.concatenate([nothing, below], axis=0).T
    lane = lax.broadcasted_iota(jnp.int32, (1, WIDTH), 1)
    inner = [weights[:, :WIDTH], weights[:, WIDTH:]]
    for copy in copies:
        copy.wait()

    @pl.when(is_two == 1)
    def _():
        for copy in two_copies:
            copy.wait()

    step = rows // 5
    for n in range(5):
        here = slice(n * step, (n + 1) * step)
        odd_sum = sums_ref[0, here] + sums_ref[1, here]
        even_sum = jnp.where(
            is_two == 1, sums_ref[2, here] + sums_ref[3, here], zero_ref[here] + zero_got_ref[here]
        )
        left = jnp.where(odd == 0, odd_sum, even_sum)
        right = jnp.where(odd == 0, even_sum, odd_sum)
        made = [sides_ref[0, here] + inner[0][2:3] * left, sides_ref[1, here] + inner[1][2:3] * right]
        for far in (1, 2):
            left_back, right_back = pltpu.roll(left, far, 1), pltpu.roll(right, far, 1)
            left_on, right_on = pltpu.roll(left, WIDTH - far, 1), pltpu.roll(right, WIDTH - far, 1)
            back, on = [w[2 - far : 3 - far] for w in inner], [w[2 + far : 3 + far] for w in inner]
            made[0] += jnp.where(lane >= far, back[0], 0.0) * left_back
            made[0] += on[0] * jnp.where(lane < WIDTH - far, left_on, right_on)
            made[1] += back[1] * jnp.where(lane >= far, right_back, left_back)
            made[1] += jnp.where(lane < WIDTH - far, on[1], 0.0) * right_on
        out_ref[here, :WIDTH] = made[0]
        out_ref[here, WIDTH:] = made[1]
        pltpu.make_async_copy(out_ref.at[here], out_any.at[here], out_sems.at[n]).start()
    for n in range(5):
        here = slice(n * step, (n + 1) * step)
        pltpu.make_async_copy(out_ref.at[here], out_any.at[here], out_sems.at[n]).wait()


def flags_of(*values):
    return jnp.stack([jnp.asarray(v, jnp.int32) for v in values])


def tied(value, *others):
    return lax.optimization_barrier((value, *others))[0]


def by_ring(relation, effects, phi_one, phi_two, innov_scale):
    gens, tms = lax.axis_size("gen"), lax.axis_size("tm")
    share = gens // tms
    half = gens // 2
    rows, depth = relation.shape
    cut = depth // 256 * 128
    wide = pl.cdiv(rows, 128) * 128
    order = list(range(0, gens, 2)) + list(range(gens - 1, 0, -2))
    forward = [(order[p], order[(p + 1) % gens]) for p in range(gens)]
    backward = [(b, a) for a, b in forward]
    swap = [(t, t ^ 1) for t in range(tms)]
    gen, tm = lax.axis_index("gen"), lax.axis_index("tm")

    def place_of(g):
        return jnp.where(g % 2 == 0, g // 2, gens - 1 - g // 2)

    place = place_of(gen)

    def block_at(far):
        p = (place + far + gens) % gens
        return jnp.where(p < half, 2 * p, 2 * (gens - 1 - p) + 1)

    def owner_of(far):
        return block_at(far) // share

    def ahead_of(x):
        return lax.ppermute(x, "gen", backward)

    def behind_of(x):
        return lax.ppermute(x, "gen", forward)

    def multiplied(*fars, after=(), cost=1):
        parts = [tied(x, *after) for far in fars for x in blocks[far]]
        made = call(
            products_kernel,
            [(rows, WIDTH), (4, wide)] * len(fars),
            (relation, *parts),
            [pltpu.VMEM((rows, 2 * WIDTH), jnp.float32), pltpu.VMEM((wide, WIDTH), jnp.float32)],
            flops=cost * len(fars) * KERNEL_FLOPS,
        )
        for n, far in enumerate(fars):
            products[far], edges[far] = made[2 * n : 2 * n + 2]

    def over_cores(x, pieces=1):
        piece = x.shape[0] // pieces
        return [lax.ppermute(x[n * piece : (n + 1) * piece], "tm", swap) for n in range(pieces)]

    def keeps(far):
        return owner_of(far) % 2 == tm % 2

    def paired(*fars):
        return call(
            pairs_kernel,
            [(len(fars) * rows, WIDTH)] * 2,
            [products[f] for far in fars for f in (far, far + half if far <= 0 else far - half)],
            (),
            (flags_of(*[keeps(far) for far in fars]),),
            flops=KERNEL_FLOPS // 2,
        )

    def over_y_of(fars, x):
        across = [
            (g * tms + (t ^ 2), g * tms + t)
            for far in fars
            for p, g in enumerate(order)
            for t in [order[(p + far) % gens] // share]
        ]
        return lax.ppermute(x, ("gen", "tm"), across)

    def over_y(x):
        return lax.ppermute(x, "tm", [(t, t ^ 2) for t in range(tms)])

    top, bottom = effects[:cut], effects[cut:]
    blocks, products, edges = {0: (top, bottom)}, {}, {}
    behind, ahead = blocks[0], blocks[0]
    multiplied(0)
    for n in range(1, half):
        behind_top = behind_of(behind[0] if n < 3 else tied(behind[0], products[n - 2]))
        ahead_bottom = ahead_of(ahead[1])
        behind_bottom = behind_of(behind[1])
        ahead_top = ahead_of(ahead[0])
        behind, ahead = (behind_top, behind_bottom), (ahead_top, ahead_bottom)
        blocks[-n], blocks[n] = behind, ahead
        if n < half - 1:
            multiplied(-n, n)
    blocks[half] = (behind_of(behind[0]), ahead_of(ahead[1]))
    send, keep = paired(-2)
    two_sum = keep + over_cores(send)[0]
    two_got = over_y_of((-2, 2), two_sum)
    multiplied(1 - half, half - 1)
    send, keep = paired(-1, 1)
    odd_owner = jnp.where(keeps(-1), owner_of(-1), owner_of(3))
    odd_send, odd_sum = call(
        part_sums_kernel,
        [(rows, WIDTH)] * 2,
        (keep, *over_cores(send, CORE_PIECES)),
        scalars=(flags_of(odd_owner // 2 != tm // 2),),
        flops=KERNEL_FLOPS // 2,
    )
    odd_got = over_y(odd_send)
    multiplied(half, cost=LAST_COST)
    products[-half] = products[half]
    send, keep = paired(0)
    fars = sorted(edges)
    at = []
    for owner in (1 - tm % 2, 3 - tm % 2, tm % 2, 2 + tm % 2):
        for g, there in ((share * owner - 1, owner > 0), (share * owner + share, owner < tms - 1)):
            index = (place_of(g) - place + gens + half - 1) % gens
            at.append(jnp.where(there, index, len(fars)))
    border_send, border_keep = call(
        borders_kernel,
        [(8, wide)] * 2,
        [edges[far] for far in fars],
        [pltpu.VMEM((len(fars) + 1, 4, wide), jnp.float32)],
        (flags_of(*at),),
        flops=KERNEL_FLOPS // 10,
    )
    border_send, border_sum = call(
        border_sums_kernel,
        [(4, wide)] * 2,
        (border_keep, over_cores(border_send)[0]),
        scalars=(flags_of(tm // 2),),
        flops=KERNEL_FLOPS // 10,
    )
    border_got = over_y(border_send)
    zero_sum = tied(keep, two_got) + over_cores(send)[0]
    zero_got = over_y_of((0, half), zero_sum)
    weights = call(weights_kernel, [(8, phi_one.shape[0])], (phi_one, phi_two, innov_scale))[0]
    odd_column = (place_of(share * tm) - place) % 2 == 0
    is_two = (owner_of(2) == tm) | (owner_of(-2) == tm)
    return call(
        last_kernel,
        [(rows, share * WIDTH)],
        (odd_sum, odd_got, two_sum, two_got, zero_sum, zero_got, border_sum, border_got, weights),
        [
            pltpu.VMEM((4, rows, WIDTH), jnp.float32),
            pltpu.VMEM((2, wide, WIDTH), jnp.float32),
            pltpu.VMEM((rows, share * WIDTH), jnp.float32),
            pltpu.SemaphoreType.DMA((4,)),
            pltpu.SemaphoreType.DMA((5,)),
        ],
        (flags_of(odd_column, is_two, tm),),
        [ANYWHERE] * 4 + [WHOLE] * 5,
        ANYWHERE,
    )[0]


def extended(cells, sides, width):
    for axis, dim in sides:
        count = lax.axis_size(axis)
        ends = count - 1
        head = lax.slice_in_dim(cells, 0, width, axis=dim)
        tail = lax.slice_in_dim(cells, cells.shape[dim] - width, cells.shape[dim], axis=dim)
        cells = jnp.concatenate(
            [
                lax.ppermute(tail, axis, [(i, (i + 1) % count) for i in range(ends)]),
                cells,
                lax.ppermute(head, axis, [((i + 1) % count, i) for i in range(ends)]),
            ],
            axis=dim,
        )
    return cells


def temporal_block(widened, first_time, phi_one, phi_two, innov_scale):
    block = widened.shape[1] - 4
    zero_pair = jnp.zeros((2,), jnp.float32)
    first_pad = jnp.concatenate([phi_one, zero_pair])
    second_pad = jnp.concatenate([phi_two, zero_pair])
    scale_pad = jnp.concatenate([innov_scale, zero_pair])
    first_win = lax.dynamic_slice_in_dim(first_pad, first_time, block + 2)
    second_win = lax.dynamic_slice_in_dim(second_pad, first_time, block + 2)
    scale_win = lax.dynamic_slice_in_dim(scale_pad, first_time, block + 2)
    innov = (
        widened[:, 2:]
        - first_win[None, :] * widened[:, 1:-1]
        - second_win[None, :] * widened[:, :-2]
    )
    weighted = scale_win[None, :] * innov
    first_next = lax.dynamic_slice_in_dim(first_pad, first_time + 1, block)
    second_next = lax.dynamic_slice_in_dim(second_pad, first_time + 2, block)
    return (
        weighted[:, :block]
        - first_next[None, :] * weighted[:, 1 : block + 1]
        - second_next[None, :] * weighted[:, 2 : block + 2]
    )


def by_gather(relation, effects, phi_one, phi_two, innov_scale):
    relation_wide = relation.astype(jnp.float32)
    partial_sums = jnp.dot(
        relation_wide,
        lax.all_gather(effects, "gen", axis=1, tiled=True),
        precision=lax.Precision.HIGHEST,
        preferred_element_type=jnp.float32,
    )
    genetic = lax.psum_scatter(partial_sums, "tm", scatter_dimension=1, tiled=True)
    widened_time = extended(genetic, (("tm", 1),), 2)
    start_tm = lax.axis_index("tm") * genetic.shape[1]
    return temporal_block(widened_time, start_tm, phi_one, phi_two, innov_scale)


def on_device(relation, effects, phi_one, phi_two, innov_scale):
    gens, tms = lax.axis_size("gen"), lax.axis_size("tm")
    fits = gens == 8 and tms == 4 and effects.shape[1] == WIDTH and effects.shape[0] % 64 == 0 and relation.shape[0] % 40 == 0
    way = by_ring if fits else by_gather
    return way(relation, effects, phi_one, phi_two, innov_scale)


def solution(mesh):
    placed = (P("gen", "tm"), P("tm", "gen"), P(), P(), P())
    return jax.shard_map(
        on_device, mesh=mesh, in_specs=placed, out_specs=P("gen", "tm"), check_vma=False
    )
```

```python
import functools

import jax
import jax.numpy as jnp
from jax import lax
from jax.experimental import pallas as pl
from jax.experimental.pallas import tpu as pltpu
from jax.sharding import PartitionSpec as P

VMEM_LIMIT = 12 * 1024 * 1024
WIDTH = 128
KERNEL_FLOPS = 10**8

WHOLE = pl.BlockSpec(memory_space=pltpu.VMEM)


def call(kernel, shapes, operands, scratch=(), flops=0):
    return pl.pallas_call(
        kernel,
        out_shape=[jax.ShapeDtypeStruct(shape, jnp.float32) for shape in shapes],
        in_specs=[WHOLE] * len(operands),
        out_specs=[WHOLE] * len(shapes),
        scratch_shapes=scratch,
        compiler_params=pltpu.CompilerParams(vmem_limit_bytes=VMEM_LIMIT),
        cost_estimate=pl.CostEstimate(flops=flops, bytes_accessed=0, transcendentals=0),
    )(*operands)


def bands(phi_one, phi_two, innov_scale):
    count = phi_one.shape[1]
    row = lax.broadcasted_iota(jnp.int32, (8, count), 0)
    lane = lax.broadcasted_iota(jnp.int32, (8, count), 1)

    def rows(*values):
        out = jnp.zeros((8, count), jnp.float32)
        for n, value in enumerate(values):
            out = jnp.where(row == n, value, out)
        return out

    now = rows(phi_one, phi_two, innov_scale)
    next_1 = jnp.where(lane < count - 1, pltpu.roll(now, count - 1, 1), 0.0)
    next_2 = jnp.where(lane < count - 2, pltpu.roll(now, count - 2, 1), 0.0)
    first_0, second_0, scale_0 = (now[n : n + 1] for n in range(3))
    first_1, second_1, scale_1 = (next_1[n : n + 1] for n in range(3))
    first_2, second_2, scale_2 = (next_2[n : n + 1] for n in range(3))
    return rows(
        -scale_0 * second_0,
        first_1 * scale_1 * second_1 - scale_0 * first_0,
        scale_0 + first_1 * first_1 * scale_1 + second_2 * second_2 * scale_2,
        second_2 * scale_2 * first_2 - first_1 * scale_1,
        -second_2 * scale_2,
    )


class Spot:
    def __init__(self, gens, tms):
        self.gens, self.share, self.half = gens, gens // tms, gens // 2
        self.gen, self.tm = lax.axis_index("gen"), lax.axis_index("tm")
        self.place = self.place_of(self.gen)

    def place_of(self, gen):
        return jnp.where(gen % 2 == 0, gen // 2, self.gens - 1 - gen // 2)

    def block_at(self, far):
        p = (self.place + (far + self.gens)) % self.gens
        return jnp.where(p < self.half, 2 * p, 2 * (self.gens - 1 - p) + 1)

    def owner_of(self, far):
        return self.block_at(far) // self.share

    def keeps(self, far):
        return jnp.where(self.owner_of(far) % 2 == self.tm % 2, 1, 0)

    def border_of(self, far, fars):
        there = (2 * self.gens - 2 * self.place - far) % self.gens
        at = jnp.int32(len(fars))
        for m, other in enumerate(fars):
            if other != far:
                at = jnp.where(there == other % self.gens, m, at)
        return at


def weights_kernel(one_ref, two_ref, scale_ref, weights_ref):
    weights_ref[...] = bands(one_ref[...][None], two_ref[...][None], scale_ref[...][None])


def products_kernel(relation_ref, *refs):
    both_ref, padded_ref = refs[-2:]
    count = (len(refs) - 2) // 4
    rows = relation_ref.shape[0]
    padded_ref[...] = jnp.zeros_like(padded_ref)
    for n in range(count):
        block = jnp.concatenate([refs[2 * n][...], refs[2 * n + 1][...]], axis=0)
        high = block.astype(jnp.bfloat16)
        low = (block - high.astype(jnp.float32)).astype(jnp.bfloat16)
        both_ref[...] = jnp.dot(
            relation_ref[...],
            jnp.concatenate([high, low], axis=1),
            preferred_element_type=jnp.float32,
        )
        padded_ref[:rows] = both_ref[:, :WIDTH] + both_ref[:, WIDTH:]
        refs[2 * count + 2 * n][...] = padded_ref[:rows]
        turned = padded_ref[...].T
        edges_ref = refs[2 * count + 2 * n + 1]
        edges_ref[0:2] = turned[0:2]
        edges_ref[2:4] = turned[WIDTH - 2 :]


def class_kernel(spot_of, fars, *refs):
    send_ref, keep_ref, edges_ref, message_ref = refs[-4:]
    spot = spot_of()
    rows, long = refs[0].shape[0], message_ref.shape[1]
    for m in range(4):
        edges_ref[m] = refs[2 * m + 1][...]
    edges_ref[4] = jnp.zeros_like(refs[1])
    for m in range(4):
        there = edges_ref[spot.border_of(fars[m], fars)]
        border = jnp.where(spot.block_at(fars[m]) % spot.share == 0, there[2:4], there[0:2])
        message_ref[m % 2, :rows] = refs[2 * m][...]
        message_ref[m % 2, rows:] = jnp.zeros((long - rows, WIDTH), jnp.float32)
        for k in range(border.shape[1] // WIDTH):
            message_ref[m % 2, rows + 2 * k : rows + 2 * k + 2] = border[:, k * WIDTH : (k + 1) * WIDTH]
        if m % 2:
            here = pl.ds(m // 2 * long, long)
            near = spot.keeps(fars[m - 1])
            keep_ref[here] = message_ref[1 - near]
            send_ref[here] = message_ref[near]


def part_sums_kernel(spot_of, fars, keep_ref, got_ref, send_ref, mine_ref):
    spot = spot_of()
    owner = jnp.where(spot.keeps(fars[0]) == 1, spot.owner_of(fars[0]), spot.owner_of(fars[1]))
    mine = jnp.where(owner // 2 == spot.tm // 2, 0, 1)
    rows = mine_ref.shape[0]
    for n in range(2):

        @pl.when(mine == n)
        def _():
            here, there = slice(n * rows, (n + 1) * rows), slice((1 - n) * rows, (2 - n) * rows)
            send_ref[...] = keep_ref[there] + got_ref[there]
            mine_ref[...] = keep_ref[here] + got_ref[here]


def last_kernel(
    spot_of, mine_odd, got_odd, mine_even, got_even, weights_ref, out_ref, sums_ref, sides_ref
):
    spot = spot_of()
    odd = jnp.where((spot.place_of(spot.share * spot.tm) + spot.place) % 2 == 0, 1, 0)
    rows = out_ref.shape[0]
    span = sides_ref.shape[1]
    sums_ref[odd] = mine_odd[...] + got_odd[...]
    sums_ref[1 - odd] = mine_even[...] + got_even[...]
    start = pl.multiple_of(spot.tm * (2 * WIDTH), 2 * WIDTH)
    weights = weights_ref[:, pl.ds(start, 2 * WIDTH)]
    row = lax.broadcasted_iota(jnp.int32, (8, span), 0)
    nothing = jnp.zeros((WIDTH - 8, span), jnp.float32)

    def border(column):
        return jnp.concatenate(
            [sums_ref[column, rows + 2 * k : rows + 2 * k + 2] for k in range(span // WIDTH)], axis=1
        )

    before, after = border(0), border(1)
    end = 2 * WIDTH - 1
    first = weights[0:1, 0:1] * before[0:1] + weights[1:2, 0:1] * before[1:2]
    second = weights[0:1, 1:2] * before[1:2]
    above = jnp.where(row == 0, first, jnp.where(row == 1, second, 0.0))
    last = weights[3:4, end:] * after[0:1] + weights[4:5, end:] * after[1:2]
    but_last = weights[4:5, end - 1 : end] * after[0:1]
    below = jnp.where(row == 7, last, jnp.where(row == 6, but_last, 0.0))
    sides_ref[0] = jnp.concatenate([above, nothing], axis=0).T
    sides_ref[1] = jnp.concatenate([nothing, below], axis=0).T
    lane = lax.broadcasted_iota(jnp.int32, (1, WIDTH), 1)
    inner = [weights[:, :WIDTH], weights[:, WIDTH:]]
    step = rows // 5

    @pl.loop(0, 5)
    def _(n):
        here = pl.ds(pl.multiple_of(n * step, 8), step)
        left, right = sums_ref[0, here], sums_ref[1, here]
        made = [sides_ref[0, here] + inner[0][2:3] * left, sides_ref[1, here] + inner[1][2:3] * right]
        for far in (1, 2):
            left_back, right_back = pltpu.roll(left, far, 1), pltpu.roll(right, far, 1)
            left_on, right_on = pltpu.roll(left, WIDTH - far, 1), pltpu.roll(right, WIDTH - far, 1)
            back, on = [w[2 - far : 3 - far] for w in inner], [w[2 + far : 3 + far] for w in inner]
            made[0] += jnp.where(lane >= far, back[0], 0.0) * left_back
            made[0] += on[0] * jnp.where(lane < WIDTH - far, left_on, right_on)
            made[1] += back[1] * jnp.where(lane >= far, right_back, left_back)
            made[1] += jnp.where(lane < WIDTH - far, on[1], 0.0) * right_on
        out_ref[here, :WIDTH] = made[0]
        out_ref[here, WIDTH:] = made[1]


def tied(value, *others):
    return lax.optimization_barrier((value, *others))[0]


def by_ring(relation, effects, phi_one, phi_two, innov_scale):
    gens, tms = lax.axis_size("gen"), lax.axis_size("tm")
    share = gens // tms
    half = gens // 2
    rows, depth = relation.shape
    cut = depth // 256 * 128
    wide = pl.cdiv(rows, 128) * 128
    long = rows + pl.cdiv(2 * wide // 128, 8) * 8
    order = list(range(0, gens, 2)) + list(range(gens - 1, 0, -2))
    forward = [(order[p], order[(p + 1) % gens]) for p in range(gens)]
    backward = [(b, a) for a, b in forward]
    swap = [(t, t ^ 1) for t in range(tms)]
    def spot_of():
        return Spot(gens, tms)

    def ahead_of(x):
        return lax.ppermute(x, "gen", backward)

    def behind_of(x):
        return lax.ppermute(x, "gen", forward)

    def multiplied(*fars, after=()):
        parts = [tied(x, *after) for far in fars for x in blocks[far]]
        made = call(
            products_kernel,
            [(rows, WIDTH), (4, wide)] * len(fars),
            (relation, *parts),
            [pltpu.VMEM((rows, 2 * WIDTH), jnp.float32), pltpu.VMEM((wide, WIDTH), jnp.float32)],
            flops=len(fars) * KERNEL_FLOPS,
        )
        for n, far in enumerate(fars):
            products[far] = made[2 * n : 2 * n + 2]

    def core_sums(fars):
        send, keep = call(
            functools.partial(class_kernel, spot_of, fars),
            [(2 * long, WIDTH)] * 2,
            [x for far in fars for x in products[far]],
            [pltpu.VMEM((5, 4, wide), jnp.float32), pltpu.VMEM((2, long, WIDTH), jnp.float32)],
            flops=KERNEL_FLOPS // 2,
        )
        return call(
            functools.partial(part_sums_kernel, spot_of, fars),
            [(long, WIDTH)] * 2,
            (keep, lax.ppermute(send, "tm", swap)),
            flops=KERNEL_FLOPS // 2,
        )

    def over_y(x):
        return lax.ppermute(x, "tm", [(t, t ^ 2) for t in range(tms)])

    top, bottom = effects[:cut], effects[cut:]
    blocks, products = {0: (top, bottom)}, {}
    behind, ahead = blocks[0], blocks[0]
    multiplied(0)
    for n in range(1, half):
        behind_top = behind_of(behind[0] if n < 3 else tied(behind[0], *products[n - 2]))
        ahead_bottom = ahead_of(ahead[1])
        behind_bottom = behind_of(behind[1])
        ahead_top = ahead_of(ahead[0])
        behind, ahead = (behind_top, behind_bottom), (ahead_top, ahead_bottom)
        blocks[-n], blocks[n] = behind, ahead
        if n < half - 1:
            multiplied(-n, n)
    blocks[half] = (behind_of(behind[0]), ahead_of(ahead[1]))
    multiplied(1 - half, half - 1, after=(*products[half - 2],))
    odd_send, odd_mine = core_sums((-1, 3, 1, -3))
    odd_got = over_y(odd_send)
    multiplied(half, after=(odd_got,))
    even_send, even_mine = core_sums((0, 4, 2, -2))
    even_got = over_y(even_send)
    weights = call(weights_kernel, [(8, phi_one.shape[0])], (phi_one, phi_two, innov_scale))[0]
    return call(
        functools.partial(last_kernel, spot_of),
        [(rows, share * WIDTH)],
        (odd_mine, odd_got, even_mine, even_got, weights),
        [pltpu.VMEM((2, long, WIDTH), jnp.float32), pltpu.VMEM((2, wide, WIDTH), jnp.float32)],
    )[0]


def extended(cells, sides, width):
    for axis, dim in sides:
        count = lax.axis_size(axis)
        ends = count - 1
        head = lax.slice_in_dim(cells, 0, width, axis=dim)
        tail = lax.slice_in_dim(cells, cells.shape[dim] - width, cells.shape[dim], axis=dim)
        cells = jnp.concatenate(
            [
                lax.ppermute(tail, axis, [(i, (i + 1) % count) for i in range(ends)]),
                cells,
                lax.ppermute(head, axis, [((i + 1) % count, i) for i in range(ends)]),
            ],
            axis=dim,
        )
    return cells


def temporal_block(widened, first_time, phi_one, phi_two, innov_scale):
    block = widened.shape[1] - 4
    zero_pair = jnp.zeros((2,), jnp.float32)
    first_pad = jnp.concatenate([phi_one, zero_pair])
    second_pad = jnp.concatenate([phi_two, zero_pair])
    scale_pad = jnp.concatenate([innov_scale, zero_pair])
    first_win = lax.dynamic_slice_in_dim(first_pad, first_time, block + 2)
    second_win = lax.dynamic_slice_in_dim(second_pad, first_time, block + 2)
    scale_win = lax.dynamic_slice_in_dim(scale_pad, first_time, block + 2)
    innov = (
        widened[:, 2:]
        - first_win[None, :] * widened[:, 1:-1]
        - second_win[None, :] * widened[:, :-2]
    )
    weighted = scale_win[None, :] * innov
    first_next = lax.dynamic_slice_in_dim(first_pad, first_time + 1, block)
    second_next = lax.dynamic_slice_in_dim(second_pad, first_time + 2, block)
    return (
        weighted[:, :block]
        - first_next[None, :] * weighted[:, 1 : block + 1]
        - second_next[None, :] * weighted[:, 2 : block + 2]
    )


def by_gather(relation, effects, phi_one, phi_two, innov_scale):
    relation_wide = relation.astype(jnp.float32)
    partial_sums = jnp.dot(
        relation_wide,
        lax.all_gather(effects, "gen", axis=1, tiled=True),
        precision=lax.Precision.HIGHEST,
        preferred_element_type=jnp.float32,
    )
    genetic = lax.psum_scatter(partial_sums, "tm", scatter_dimension=1, tiled=True)
    widened_time = extended(genetic, (("tm", 1),), 2)
    start_tm = lax.axis_index("tm") * genetic.shape[1]
    return temporal_block(widened_time, start_tm, phi_one, phi_two, innov_scale)


def on_device(relation, effects, phi_one, phi_two, innov_scale):
    gens, tms = lax.axis_size("gen"), lax.axis_size("tm")
    fits = gens == 8 and tms == 4 and effects.shape[1] == WIDTH and effects.shape[0] % 64 == 0 and relation.shape[0] % 40 == 0
    way = by_ring if fits else by_gather
    return way(relation, effects, phi_one, phi_two, innov_scale)


def solution(mesh):
    placed = (P("gen", "tm"), P("tm", "gen"), P(), P(), P())
    return jax.shard_map(
        on_device, mesh=mesh, in_specs=placed, out_specs=P("gen", "tm"), check_vma=False
    )
```

```python
import functools

import jax
import jax.numpy as jnp
from jax import lax
from jax.experimental import pallas as pl
from jax.experimental.pallas import tpu as pltpu
from jax.sharding import PartitionSpec as P

VMEM_LIMIT = 12 * 1024 * 1024
WIDTH = 128
KERNEL_FLOPS = 10**8

WHOLE = pl.BlockSpec(memory_space=pltpu.VMEM)


def call(kernel, shapes, operands, scratch=(), flops=0, into=WHOLE):
    return pl.pallas_call(
        kernel,
        out_shape=[jax.ShapeDtypeStruct(shape, jnp.float32) for shape in shapes],
        in_specs=[WHOLE] * len(operands),
        out_specs=[into] * len(shapes),
        scratch_shapes=scratch,
        compiler_params=pltpu.CompilerParams(vmem_limit_bytes=VMEM_LIMIT),
        cost_estimate=pl.CostEstimate(flops=flops, bytes_accessed=0, transcendentals=0),
    )(*operands)


def bands(phi_one, phi_two, innov_scale):
    count = phi_one.shape[1]
    row = lax.broadcasted_iota(jnp.int32, (8, count), 0)
    lane = lax.broadcasted_iota(jnp.int32, (8, count), 1)

    def rows(*values):
        out = jnp.zeros((8, count), jnp.float32)
        for n, value in enumerate(values):
            out = jnp.where(row == n, value, out)
        return out

    now = rows(phi_one, phi_two, innov_scale)
    next_1 = jnp.where(lane < count - 1, pltpu.roll(now, count - 1, 1), 0.0)
    next_2 = jnp.where(lane < count - 2, pltpu.roll(now, count - 2, 1), 0.0)
    first_0, second_0, scale_0 = (now[n : n + 1] for n in range(3))
    first_1, second_1, scale_1 = (next_1[n : n + 1] for n in range(3))
    first_2, second_2, scale_2 = (next_2[n : n + 1] for n in range(3))
    return rows(
        -scale_0 * second_0,
        first_1 * scale_1 * second_1 - scale_0 * first_0,
        scale_0 + first_1 * first_1 * scale_1 + second_2 * second_2 * scale_2,
        second_2 * scale_2 * first_2 - first_1 * scale_1,
        -second_2 * scale_2,
    )


class Spot:
    def __init__(self, gens, tms):
        self.gens, self.share, self.half = gens, gens // tms, gens // 2
        self.gen, self.tm = lax.axis_index("gen"), lax.axis_index("tm")
        self.place = self.place_of(self.gen)

    def place_of(self, gen):
        return jnp.where(gen % 2 == 0, gen // 2, self.gens - 1 - gen // 2)

    def block_at(self, far):
        p = (self.place + (far + self.gens)) % self.gens
        return jnp.where(p < self.half, 2 * p, 2 * (self.gens - 1 - p) + 1)

    def owner_of(self, far):
        return self.block_at(far) // self.share

    def keeps(self, far):
        return jnp.where(self.owner_of(far) % 2 == self.tm % 2, 1, 0)

    def border_of(self, far, fars):
        there = (2 * self.gens - 2 * self.place - far) % self.gens
        at = jnp.int32(len(fars))
        for m, other in enumerate(fars):
            if other != far:
                at = jnp.where(there == other % self.gens, m, at)
        return at


def weights_kernel(one_ref, two_ref, scale_ref, weights_ref):
    weights_ref[...] = bands(one_ref[...][None], two_ref[...][None], scale_ref[...][None])


def products_kernel(relation_ref, *refs):
    both_ref, padded_ref = refs[-2:]
    count = (len(refs) - 2) // 4
    rows = relation_ref.shape[0]
    padded_ref[...] = jnp.zeros_like(padded_ref)
    for n in range(count):
        block = jnp.concatenate([refs[2 * n][...], refs[2 * n + 1][...]], axis=0)
        high = block.astype(jnp.bfloat16)
        low = (block - high.astype(jnp.float32)).astype(jnp.bfloat16)
        both_ref[...] = jnp.dot(
            relation_ref[...],
            jnp.concatenate([high, low], axis=1),
            preferred_element_type=jnp.float32,
        )
        padded_ref[:rows] = both_ref[:, :WIDTH] + both_ref[:, WIDTH:]
        refs[2 * count + 2 * n][...] = padded_ref[:rows]
        turned = padded_ref[...].T
        edges_ref = refs[2 * count + 2 * n + 1]
        edges_ref[0:2] = turned[0:2]
        edges_ref[2:4] = turned[WIDTH - 2 :]


def odd_kernel(spot_of, fars, *refs):
    send_ref, keep_ref, edges_ref, message_ref = refs[-4:]
    spot = spot_of()
    rows, long = refs[0].shape[0], message_ref.shape[1]
    for m in range(4):
        edges_ref[m] = refs[2 * m + 1][...]
    edges_ref[4] = jnp.zeros_like(refs[1])
    for m in range(4):
        there = edges_ref[spot.border_of(fars[m], fars)]
        border = jnp.where(spot.block_at(fars[m]) % spot.share == 0, there[2:4], there[0:2])
        message_ref[m % 2, :rows] = refs[2 * m][...]
        message_ref[m % 2, rows:] = jnp.zeros((long - rows, WIDTH), jnp.float32)
        for k in range(border.shape[1] // WIDTH):
            message_ref[m % 2, rows + 2 * k : rows + 2 * k + 2] = border[:, k * WIDTH : (k + 1) * WIDTH]
        if m % 2:
            here = pl.ds(m // 2 * long, long)
            near = spot.keeps(fars[m - 1])
            keep_ref[here] = message_ref[1 - near]
            send_ref[here] = message_ref[near]


def halves_kernel(spot_of, near, near_ref, far_ref, send_ref, keep_ref):
    spot = spot_of()
    rows = near_ref.shape[0] // 2
    core = spot.tm % 2
    mine = spot.owner_of(near) // 2 == spot.tm // 2
    for ours in (True, False):

        @pl.when(mine == ours)
        def _():
            for n, ref in enumerate((near_ref, far_ref) if ours else (far_ref, near_ref)):
                here = pl.ds(n * rows, rows)
                send_ref[here] = ref[pl.ds(pl.multiple_of((1 - core) * rows, 8), rows)]
                keep_ref[here] = ref[pl.ds(pl.multiple_of(core * rows, 8), rows)]


def half_sums_kernel(keep_ref, got_ref, send_ref, mine_ref):
    rows = mine_ref.shape[0]
    mine_ref[...] = keep_ref[:rows] + got_ref[:rows]
    send_ref[...] = keep_ref[rows:] + got_ref[rows:]


def chip_pair_kernel(spot_of, near, near_ref, far_ref, send_ref, keep_ref):
    spot = spot_of()
    mine = spot.owner_of(near) // 2 == spot.tm // 2

    @pl.when(mine)
    def _():
        keep_ref[...] = near_ref[...]
        send_ref[...] = far_ref[...]

    @pl.when(jnp.logical_not(mine))
    def _():
        keep_ref[...] = far_ref[...]
        send_ref[...] = near_ref[...]


def borders_kernel(spot_of, fars, *refs):
    send_ref, keep_ref, edges_ref = refs[-3:]
    spot = spot_of()
    for m in range(4):
        edges_ref[m] = refs[m][...]
    edges_ref[4] = jnp.zeros_like(refs[0])
    chip, core = spot.tm // 2, spot.tm % 2
    send_ref[...] = jnp.zeros_like(send_ref)
    keep_ref[...] = jnp.zeros_like(keep_ref)
    for m, far in enumerate(fars):
        owner = spot.owner_of(far)
        there = edges_ref[spot.border_of(far, fars)]
        border = jnp.where(spot.block_at(far) % spot.share == 0, there[2:4], there[0:2])
        for n in range(2):
            for out_ref, whose in ((send_ref, 1 - core), (keep_ref, core)):
                wanted = 2 * jnp.where(n == 0, chip, 1 - chip) + whose

                @pl.when(owner == wanted)
                def _():
                    out_ref[2 * n : 2 * n + 2] = border


def border_sums_kernel(keep_ref, got_ref, send_ref, mine_ref):
    mine_ref[...] = keep_ref[0:2] + got_ref[0:2]
    send_ref[...] = keep_ref[2:4] + got_ref[2:4]


def sum_kernel(one_ref, other_ref, out_ref):
    out_ref[...] = one_ref[...] + other_ref[...]


def part_sums_kernel(spot_of, fars, keep_ref, got_ref, send_ref, mine_ref):
    spot = spot_of()
    owner = jnp.where(spot.keeps(fars[0]) == 1, spot.owner_of(fars[0]), spot.owner_of(fars[1]))
    mine = jnp.where(owner // 2 == spot.tm // 2, 0, 1)
    rows = mine_ref.shape[0]
    for n in range(2):

        @pl.when(mine == n)
        def _():
            here, there = slice(n * rows, (n + 1) * rows), slice((1 - n) * rows, (2 - n) * rows)
            send_ref[...] = keep_ref[there] + got_ref[there]
            mine_ref[...] = keep_ref[here] + got_ref[here]


def last_kernel(
    spot_of,
    mine_odd,
    got_odd,
    two_sum,
    two_got,
    zero_sum,
    zero_got,
    border_mine,
    border_got,
    weights_ref,
    out_any,
    sums_ref,
    sides_ref,
    made_ref,
    sems,
):
    spot = spot_of()
    odd = jnp.where((spot.place_of(spot.share * spot.tm) + spot.place) % 2 == 0, 1, 0)
    rows = out_any.shape[0]
    span = sides_ref.shape[1]
    is_two = (spot.owner_of(2) == spot.tm) | (spot.owner_of(-2) == spot.tm)
    sums_ref[odd] = mine_odd[:rows] + got_odd[:rows]

    @pl.when(is_two)
    def _():
        sums_ref[1 - odd] = two_sum[...] + two_got[...]

    @pl.when(jnp.logical_not(is_two))
    def _():
        half, core = rows // 2, spot.tm % 2
        sums_ref[1 - odd, pl.ds(pl.multiple_of(core * half, 8), half)] = zero_sum[...]
        sums_ref[1 - odd, pl.ds(pl.multiple_of((1 - core) * half, 8), half)] = zero_got[...]

    start = pl.multiple_of(spot.tm * (2 * WIDTH), 2 * WIDTH)
    weights = weights_ref[:, pl.ds(start, 2 * WIDTH)]
    row = lax.broadcasted_iota(jnp.int32, (8, span), 0)
    nothing = jnp.zeros((WIDTH - 8, span), jnp.float32)

    extra = mine_odd[rows:] + got_odd[rows:]
    odd_border = jnp.concatenate([extra[2 * k : 2 * k + 2] for k in range(span // WIDTH)], axis=1)
    even_border = border_mine[...] + border_got[...]
    before = jnp.where(odd == 0, odd_border, even_border)
    after = jnp.where(odd == 0, even_border, odd_border)
    end = 2 * WIDTH - 1
    first = weights[0:1, 0:1] * before[0:1] + weights[1:2, 0:1] * before[1:2]
    second = weights[0:1, 1:2] * before[1:2]
    above = jnp.where(row == 0, first, jnp.where(row == 1, second, 0.0))
    last = weights[3:4, end:] * after[0:1] + weights[4:5, end:] * after[1:2]
    but_last = weights[4:5, end - 1 : end] * after[0:1]
    below = jnp.where(row == 7, last, jnp.where(row == 6, but_last, 0.0))
    sides_ref[0] = jnp.concatenate([above, nothing], axis=0).T
    sides_ref[1] = jnp.concatenate([nothing, below], axis=0).T
    lane = lax.broadcasted_iota(jnp.int32, (1, WIDTH), 1)
    inner = [weights[:, :WIDTH], weights[:, WIDTH:]]
    near = [jnp.where(lane >= far, inner[0][2 - far : 3 - far], 0.0) for far in (1, 2)]
    beyond = [jnp.where(lane < WIDTH - far, inner[1][2 + far : 3 + far], 0.0) for far in (1, 2)]
    pieces = 5
    step = rows // pieces
    copies = []
    for n in range(pieces):
        here = slice(n * step, (n + 1) * step)
        left, right = sums_ref[0, here], sums_ref[1, here]
        made_left = sides_ref[0, here] + inner[0][2:3] * left
        made_right = sides_ref[1, here] + inner[1][2:3] * right
        for far in (1, 2):
            left_back, right_back = pltpu.roll(left, far, 1), pltpu.roll(right, far, 1)
            left_on, right_on = pltpu.roll(left, WIDTH - far, 1), pltpu.roll(right, WIDTH - far, 1)
            on = jnp.where(lane < WIDTH - far, left_on, right_on)
            back = jnp.where(lane >= far, right_back, left_back)
            made_left += near[far - 1] * left_back + inner[0][2 + far : 3 + far] * on
            made_right += inner[1][2 - far : 3 - far] * back + beyond[far - 1] * right_on
        made_ref[here, :WIDTH] = made_left
        made_ref[here, WIDTH:] = made_right
        copies.append(pltpu.make_async_copy(made_ref.at[here], out_any.at[here], sems.at[n]))
        copies[n].start()
    for copy in copies:
        copy.wait()


def tied(value, *others):
    return lax.optimization_barrier((value, *others))[0]


def by_ring(relation, effects, phi_one, phi_two, innov_scale):
    gens, tms = lax.axis_size("gen"), lax.axis_size("tm")
    share = gens // tms
    half = gens // 2
    rows, depth = relation.shape
    cut = depth // 256 * 128
    wide = pl.cdiv(rows, 128) * 128
    long = rows + pl.cdiv(2 * wide // 128, 8) * 8
    order = list(range(0, gens, 2)) + list(range(gens - 1, 0, -2))
    forward = [(order[p], order[(p + 1) % gens]) for p in range(gens)]
    backward = [(b, a) for a, b in forward]
    swap = [(t, t ^ 1) for t in range(tms)]
    def spot_of():
        return Spot(gens, tms)

    def ahead_of(x):
        return lax.ppermute(x, "gen", backward)

    def behind_of(x):
        return lax.ppermute(x, "gen", forward)

    def multiplied(*fars, after=(), cost=1):
        parts = [tied(x, *after) for far in fars for x in blocks[far]]
        made = call(
            products_kernel,
            [(rows, WIDTH), (4, wide)] * len(fars),
            (relation, *parts),
            [pltpu.VMEM((rows, 2 * WIDTH), jnp.float32), pltpu.VMEM((wide, WIDTH), jnp.float32)],
            flops=cost * len(fars) * KERNEL_FLOPS,
        )
        for n, far in enumerate(fars):
            products[far] = made[2 * n : 2 * n + 2]

    def over_cores(x):
        return lax.ppermute(x, "tm", swap)

    def over_y(x):
        return lax.ppermute(x, "tm", [(t, t ^ 2) for t in range(tms)])

    top, bottom = effects[:cut], effects[cut:]
    blocks, products = {0: (top, bottom)}, {}
    behind, ahead = blocks[0], blocks[0]
    multiplied(0)
    for n in range(1, half):
        behind_top = behind_of(behind[0] if n < 2 else tied(behind[0], *products[n - 2]))
        ahead_bottom = ahead_of(ahead[1])
        behind_bottom = behind_of(behind[1])
        ahead_top = ahead_of(ahead[0])
        behind, ahead = (behind_top, behind_bottom), (ahead_top, ahead_bottom)
        blocks[-n], blocks[n] = behind, ahead
        if n < half - 1:
            multiplied(-n, n)
    blocks[half] = (behind_of(behind[0]), ahead_of(ahead[1]))
    two_send, two_keep = call(
        functools.partial(chip_pair_kernel, spot_of, 2),
        [(rows, WIDTH)] * 2,
        (products[2][0], products[-2][0]),
        flops=KERNEL_FLOPS // 2,
    )
    two_sum = call(sum_kernel, [(rows, WIDTH)], (two_keep, over_y(two_send)), flops=KERNEL_FLOPS // 10)[0]
    two_got = over_cores(two_sum)
    multiplied(1 - half, half - 1, cost=10)
    odd_fars = (-1, 3, 1, -3)
    send, keep = call(
        functools.partial(odd_kernel, spot_of, odd_fars),
        [(2 * long, WIDTH)] * 2,
        [tied(x, two_sum) for far in odd_fars for x in products[far]],
        [pltpu.VMEM((5, 4, wide), jnp.float32), pltpu.VMEM((2, long, WIDTH), jnp.float32)],
        flops=KERNEL_FLOPS // 2,
    )
    odd_send, odd_mine = call(
        functools.partial(part_sums_kernel, spot_of, odd_fars),
        [(long, WIDTH)] * 2,
        (keep, over_cores(send)),
        flops=KERNEL_FLOPS // 2,
    )
    odd_got = over_y(odd_send)
    multiplied(half, cost=20)
    even_fars = (0, half, 2, -2)
    border_send, border_keep = call(
        functools.partial(borders_kernel, spot_of, even_fars),
        [(4, wide)] * 2,
        [products[far][1] for far in even_fars],
        [pltpu.VMEM((5, 4, wide), jnp.float32)],
        flops=KERNEL_FLOPS // 10,
    )
    border_send, border_mine = call(
        border_sums_kernel,
        [(2, wide)] * 2,
        (border_keep, over_cores(border_send)),
        flops=KERNEL_FLOPS // 10,
    )
    border_got = over_y(border_send)
    send, keep = call(
        functools.partial(halves_kernel, spot_of, 0),
        [(rows, WIDTH)] * 2,
        [tied(products[far][0], odd_got) for far in (0, half)],
        flops=KERNEL_FLOPS // 2,
    )
    zero_send, zero_mine = call(
        half_sums_kernel,
        [(rows // 2, WIDTH)] * 2,
        (keep, over_cores(send)),
        flops=KERNEL_FLOPS // 10,
    )
    zero_sum = call(
        sum_kernel,
        [(rows // 2, WIDTH)],
        (tied(zero_mine, border_got), over_y(zero_send)),
        flops=KERNEL_FLOPS // 10,
    )[0]
    zero_got = over_cores(zero_sum)
    weights = call(weights_kernel, [(8, phi_one.shape[0])], (phi_one, phi_two, innov_scale))[0]
    return call(
        functools.partial(last_kernel, spot_of),
        [(rows, share * WIDTH)],
        (odd_mine, odd_got, two_sum, two_got, zero_sum, zero_got, border_mine, border_got, weights),
        [
            pltpu.VMEM((2, rows, WIDTH), jnp.float32),
            pltpu.VMEM((2, wide, WIDTH), jnp.float32),
            pltpu.VMEM((rows, share * WIDTH), jnp.float32),
            pltpu.SemaphoreType.DMA((5,)),
        ],
        into=pl.BlockSpec(memory_space=pl.ANY),
    )[0]


def extended(cells, sides, width):
    for axis, dim in sides:
        count = lax.axis_size(axis)
        ends = count - 1
        head = lax.slice_in_dim(cells, 0, width, axis=dim)
        tail = lax.slice_in_dim(cells, cells.shape[dim] - width, cells.shape[dim], axis=dim)
        cells = jnp.concatenate(
            [
                lax.ppermute(tail, axis, [(i, (i + 1) % count) for i in range(ends)]),
                cells,
                lax.ppermute(head, axis, [((i + 1) % count, i) for i in range(ends)]),
            ],
            axis=dim,
        )
    return cells


def temporal_block(widened, first_time, phi_one, phi_two, innov_scale):
    block = widened.shape[1] - 4
    zero_pair = jnp.zeros((2,), jnp.float32)
    first_pad = jnp.concatenate([phi_one, zero_pair])
    second_pad = jnp.concatenate([phi_two, zero_pair])
    scale_pad = jnp.concatenate([innov_scale, zero_pair])
    first_win = lax.dynamic_slice_in_dim(first_pad, first_time, block + 2)
    second_win = lax.dynamic_slice_in_dim(second_pad, first_time, block + 2)
    scale_win = lax.dynamic_slice_in_dim(scale_pad, first_time, block + 2)
    innov = (
        widened[:, 2:]
        - first_win[None, :] * widened[:, 1:-1]
        - second_win[None, :] * widened[:, :-2]
    )
    weighted = scale_win[None, :] * innov
    first_next = lax.dynamic_slice_in_dim(first_pad, first_time + 1, block)
    second_next = lax.dynamic_slice_in_dim(second_pad, first_time + 2, block)
    return (
        weighted[:, :block]
        - first_next[None, :] * weighted[:, 1 : block + 1]
        - second_next[None, :] * weighted[:, 2 : block + 2]
    )


def by_gather(relation, effects, phi_one, phi_two, innov_scale):
    relation_wide = relation.astype(jnp.float32)
    partial_sums = jnp.dot(
        relation_wide,
        lax.all_gather(effects, "gen", axis=1, tiled=True),
        precision=lax.Precision.HIGHEST,
        preferred_element_type=jnp.float32,
    )
    genetic = lax.psum_scatter(partial_sums, "tm", scatter_dimension=1, tiled=True)
    widened_time = extended(genetic, (("tm", 1),), 2)
    start_tm = lax.axis_index("tm") * genetic.shape[1]
    return temporal_block(widened_time, start_tm, phi_one, phi_two, innov_scale)


def on_device(relation, effects, phi_one, phi_two, innov_scale):
    gens, tms = lax.axis_size("gen"), lax.axis_size("tm")
    fits = gens == 8 and tms == 4 and effects.shape[1] == WIDTH and effects.shape[0] % 64 == 0 and relation.shape[0] % 80 == 0
    way = by_ring if fits else by_gather
    return way(relation, effects, phi_one, phi_two, innov_scale)


def solution(mesh):
    placed = (P("gen", "tm"), P("tm", "gen"), P(), P(), P())
    return jax.shard_map(
        on_device, mesh=mesh, in_specs=placed, out_specs=P("gen", "tm"), check_vma=False
    )
```

```python
import functools

import jax
import jax.numpy as jnp
from jax import lax
from jax.experimental import pallas as pl
from jax.experimental.pallas import tpu as pltpu
from jax.sharding import PartitionSpec as P

VMEM_LIMIT = 12 * 1024 * 1024
WIDTH = 128
KERNEL_FLOPS = 10**8

WHOLE = pl.BlockSpec(memory_space=pltpu.VMEM)


def call(kernel, shapes, operands, scratch=(), flops=0, into=WHOLE):
    return pl.pallas_call(
        kernel,
        out_shape=[jax.ShapeDtypeStruct(shape, jnp.float32) for shape in shapes],
        in_specs=[WHOLE] * len(operands),
        out_specs=[into] * len(shapes),
        scratch_shapes=scratch,
        compiler_params=pltpu.CompilerParams(vmem_limit_bytes=VMEM_LIMIT),
        cost_estimate=pl.CostEstimate(flops=flops, bytes_accessed=0, transcendentals=0),
    )(*operands)


def bands(phi_one, phi_two, innov_scale):
    count = phi_one.shape[1]
    row = lax.broadcasted_iota(jnp.int32, (8, count), 0)
    lane = lax.broadcasted_iota(jnp.int32, (8, count), 1)

    def rows(*values):
        out = jnp.zeros((8, count), jnp.float32)
        for n, value in enumerate(values):
            out = jnp.where(row == n, value, out)
        return out

    now = rows(phi_one, phi_two, innov_scale)
    next_1 = jnp.where(lane < count - 1, pltpu.roll(now, count - 1, 1), 0.0)
    next_2 = jnp.where(lane < count - 2, pltpu.roll(now, count - 2, 1), 0.0)
    first_0, second_0, scale_0 = (now[n : n + 1] for n in range(3))
    first_1, second_1, scale_1 = (next_1[n : n + 1] for n in range(3))
    first_2, second_2, scale_2 = (next_2[n : n + 1] for n in range(3))
    return rows(
        -scale_0 * second_0,
        first_1 * scale_1 * second_1 - scale_0 * first_0,
        scale_0 + first_1 * first_1 * scale_1 + second_2 * second_2 * scale_2,
        second_2 * scale_2 * first_2 - first_1 * scale_1,
        -second_2 * scale_2,
    )


class Spot:
    def __init__(self, gens, tms):
        self.gens, self.share, self.half = gens, gens // tms, gens // 2
        self.gen, self.tm = lax.axis_index("gen"), lax.axis_index("tm")
        self.place = self.place_of(self.gen)

    def place_of(self, gen):
        return jnp.where(gen % 2 == 0, gen // 2, self.gens - 1 - gen // 2)

    def block_at(self, far):
        p = (self.place + (far + self.gens)) % self.gens
        return jnp.where(p < self.half, 2 * p, 2 * (self.gens - 1 - p) + 1)

    def owner_of(self, far):
        return self.block_at(far) // self.share

    def keeps(self, far):
        return jnp.where(self.owner_of(far) % 2 == self.tm % 2, 1, 0)

    def border_of(self, far, fars):
        there = (2 * self.gens - 2 * self.place - far) % self.gens
        at = jnp.int32(len(fars))
        for m, other in enumerate(fars):
            if other != far:
                at = jnp.where(there == other % self.gens, m, at)
        return at


def weights_kernel(one_ref, two_ref, scale_ref, weights_ref):
    weights_ref[...] = bands(one_ref[...][None], two_ref[...][None], scale_ref[...][None])


def products_kernel(relation_ref, *refs):
    both_ref, padded_ref = refs[-2:]
    count = (len(refs) - 2) // 4
    rows = relation_ref.shape[0]
    padded_ref[...] = jnp.zeros_like(padded_ref)
    for n in range(count):
        block = jnp.concatenate([refs[2 * n][...], refs[2 * n + 1][...]], axis=0)
        high = block.astype(jnp.bfloat16)
        low = (block - high.astype(jnp.float32)).astype(jnp.bfloat16)
        both_ref[...] = jnp.dot(
            relation_ref[...],
            jnp.concatenate([high, low], axis=1),
            preferred_element_type=jnp.float32,
        )
        padded_ref[:rows] = both_ref[:, :WIDTH] + both_ref[:, WIDTH:]
        refs[2 * count + 2 * n][...] = padded_ref[:rows]
        turned = padded_ref[...].T
        edges_ref = refs[2 * count + 2 * n + 1]
        edges_ref[0:2] = turned[0:2]
        edges_ref[2:4] = turned[WIDTH - 2 :]


def bottom_kernel(cut, relation_ref, *refs):
    both_ref = refs[-1]
    count = (len(refs) - 1) // 2
    for n in range(count):
        both_ref[...] = jnp.dot(
            relation_ref[:, cut:], two_parts(refs[n][...]), preferred_element_type=jnp.float32
        )
        refs[count + n][...] = both_ref[:, :WIDTH] + both_ref[:, WIDTH:]


def top_kernel(cut, relation_ref, *refs):
    both_ref, padded_ref = refs[-2:]
    count = (len(refs) - 2) // 4
    rows = relation_ref.shape[0]
    padded_ref[...] = jnp.zeros_like(padded_ref)
    for n in range(count):
        both_ref[...] = jnp.dot(
            relation_ref[:, :cut], two_parts(refs[n][...]), preferred_element_type=jnp.float32
        )
        padded_ref[:rows] = both_ref[:, :WIDTH] + both_ref[:, WIDTH:] + refs[count + n][...]
        refs[2 * count + 2 * n][...] = padded_ref[:rows]
        turned = padded_ref[...].T
        edges_ref = refs[2 * count + 2 * n + 1]
        edges_ref[0:2] = turned[0:2]
        edges_ref[2:4] = turned[WIDTH - 2 :]


def two_parts(block):
    high = block.astype(jnp.bfloat16)
    low = (block - high.astype(jnp.float32)).astype(jnp.bfloat16)
    return jnp.concatenate([high, low], axis=1)


def odd_kernel(spot_of, fars, *refs):
    send_ref, keep_ref, edges_ref, message_ref = refs[-4:]
    spot = spot_of()
    rows, long = refs[0].shape[0], message_ref.shape[1]
    for m in range(4):
        edges_ref[m] = refs[2 * m + 1][...]
    edges_ref[4] = jnp.zeros_like(refs[1])
    for m in range(4):
        there = edges_ref[spot.border_of(fars[m], fars)]
        border = jnp.where(spot.block_at(fars[m]) % spot.share == 0, there[2:4], there[0:2])
        message_ref[m % 2, :rows] = refs[2 * m][...]
        message_ref[m % 2, rows:] = jnp.zeros((long - rows, WIDTH), jnp.float32)
        for k in range(border.shape[1] // WIDTH):
            message_ref[m % 2, rows + 2 * k : rows + 2 * k + 2] = border[:, k * WIDTH : (k + 1) * WIDTH]
        if m % 2:
            here = pl.ds(m // 2 * long, long)
            near = spot.keeps(fars[m - 1])
            keep_ref[here] = message_ref[1 - near]
            send_ref[here] = message_ref[near]


def halves_kernel(spot_of, near, near_ref, far_ref, send_ref, keep_ref):
    spot = spot_of()
    rows = near_ref.shape[0] // 2
    core = spot.tm % 2
    mine = spot.owner_of(near) // 2 == spot.tm // 2
    for ours in (True, False):

        @pl.when(mine == ours)
        def _():
            for n, ref in enumerate((near_ref, far_ref) if ours else (far_ref, near_ref)):
                here = pl.ds(n * rows, rows)
                send_ref[here] = ref[pl.ds(pl.multiple_of((1 - core) * rows, 8), rows)]
                keep_ref[here] = ref[pl.ds(pl.multiple_of(core * rows, 8), rows)]


def half_sums_kernel(keep_ref, got_ref, send_ref, mine_ref):
    rows = mine_ref.shape[0]
    mine_ref[...] = keep_ref[:rows] + got_ref[:rows]
    send_ref[...] = keep_ref[rows:] + got_ref[rows:]


def chip_pair_kernel(spot_of, near, near_ref, far_ref, send_ref, keep_ref):
    spot = spot_of()
    mine = spot.owner_of(near) // 2 == spot.tm // 2

    @pl.when(mine)
    def _():
        keep_ref[...] = near_ref[...]
        send_ref[...] = far_ref[...]

    @pl.when(jnp.logical_not(mine))
    def _():
        keep_ref[...] = far_ref[...]
        send_ref[...] = near_ref[...]


def borders_kernel(spot_of, fars, *refs):
    send_ref, keep_ref, edges_ref = refs[-3:]
    spot = spot_of()
    for m in range(4):
        edges_ref[m] = refs[m][...]
    edges_ref[4] = jnp.zeros_like(refs[0])
    chip, core = spot.tm // 2, spot.tm % 2
    send_ref[...] = jnp.zeros_like(send_ref)
    keep_ref[...] = jnp.zeros_like(keep_ref)
    for m, far in enumerate(fars):
        owner = spot.owner_of(far)
        there = edges_ref[spot.border_of(far, fars)]
        border = jnp.where(spot.block_at(far) % spot.share == 0, there[2:4], there[0:2])
        for n in range(2):
            for out_ref, whose in ((send_ref, 1 - core), (keep_ref, core)):
                wanted = 2 * jnp.where(n == 0, chip, 1 - chip) + whose

                @pl.when(owner == wanted)
                def _():
                    out_ref[2 * n : 2 * n + 2] = border


def border_sums_kernel(keep_ref, got_ref, send_ref, mine_ref):
    mine_ref[...] = keep_ref[0:2] + got_ref[0:2]
    send_ref[...] = keep_ref[2:4] + got_ref[2:4]


def sum_kernel(one_ref, other_ref, out_ref):
    out_ref[...] = one_ref[...] + other_ref[...]


def part_sums_kernel(spot_of, fars, keep_ref, got_ref, send_ref, mine_ref):
    spot = spot_of()
    owner = jnp.where(spot.keeps(fars[0]) == 1, spot.owner_of(fars[0]), spot.owner_of(fars[1]))
    mine = jnp.where(owner // 2 == spot.tm // 2, 0, 1)
    rows = mine_ref.shape[0]
    for n in range(2):

        @pl.when(mine == n)
        def _():
            here, there = slice(n * rows, (n + 1) * rows), slice((1 - n) * rows, (2 - n) * rows)
            send_ref[...] = keep_ref[there] + got_ref[there]
            mine_ref[...] = keep_ref[here] + got_ref[here]


def row_weights(weights, far, lanes):
    return jnp.where(lanes, weights[2 + far : 3 + far], 0.0)


def beside(weights, border, left):
    span = border.shape[1]
    row = lax.broadcasted_iota(jnp.int32, (8, span), 0)
    nothing = jnp.zeros((WIDTH - 8, span), jnp.float32)
    end = WIDTH - 1
    first = weights[0:1, 0:1] * border[0:1] + weights[1:2, 0:1] * border[1:2]
    second = weights[0:1, 1:2] * border[1:2]
    above = jnp.where(row == 0, first, jnp.where(row == 1, second, 0.0))
    last = weights[3:4, end:] * border[0:1] + weights[4:5, end:] * border[1:2]
    but_last = weights[4:5, end - 1 : end] * border[0:1]
    below = jnp.where(row == 7, last, jnp.where(row == 6, but_last, 0.0))
    none = jnp.zeros_like(above)
    return jnp.concatenate(
        [jnp.where(left, above, none), nothing[: WIDTH - 16], jnp.where(left, none, below)], axis=0
    ).T


def shares(weights, other_weights, block, left):
    lane = lax.broadcasted_iota(jnp.int32, (1, WIDTH), 1)
    own = weights[2:3] * block
    beyond = 0.0
    for far in (1, 2):
        back, on = pltpu.roll(block, far, 1), pltpu.roll(block, WIDTH - far, 1)
        own += row_weights(weights, -far, lane >= far) * back
        own += row_weights(weights, far, lane < WIDTH - far) * on
        beyond += jnp.where(
            left,
            row_weights(other_weights, -far, lane < far) * back,
            row_weights(other_weights, far, lane >= WIDTH - far) * on,
        )
    return own, beyond


def odd_column(spot):
    return jnp.where((spot.place_of(spot.share * spot.tm) + spot.place) % 2 == 0, 1, 0)


def column_weights(spot, weights_ref, column):
    start = (spot.tm * 2 + column) * WIDTH
    return weights_ref[:, pl.ds(pl.multiple_of(start, WIDTH), WIDTH)]


def odd_shares_kernel(spot_of, mine_ref, got_ref, weights_ref, own_ref, beyond_ref, sides_ref):
    spot = spot_of()
    odd = odd_column(spot)
    rows, span = own_ref.shape[0], sides_ref.shape[0]
    weights = column_weights(spot, weights_ref, odd)
    others = column_weights(spot, weights_ref, 1 - odd)
    extra = mine_ref[rows:] + got_ref[rows:]
    border = jnp.concatenate([extra[2 * k : 2 * k + 2] for k in range(span // WIDTH)], axis=1)
    sides_ref[...] = beside(weights, border, odd == 0)
    step = rows // 5
    for n in range(5):
        here = slice(n * step, (n + 1) * step)
        own, beyond = shares(weights, others, mine_ref[here] + got_ref[here], odd == 0)
        own_ref[here] = own + sides_ref[here]
        beyond_ref[here] = beyond


def last_kernel(
    spot_of,
    odd_own,
    odd_beyond,
    two_sum,
    two_got,
    zero_sum,
    zero_got,
    border_mine,
    border_got,
    weights_ref,
    out_any,
    even_ref,
    sides_ref,
    made_ref,
    sems,
):
    spot = spot_of()
    odd = odd_column(spot)
    rows = out_any.shape[0]
    is_two = (spot.owner_of(2) == spot.tm) | (spot.owner_of(-2) == spot.tm)

    @pl.when(is_two)
    def _():
        even_ref[...] = two_sum[...] + two_got[...]

    @pl.when(jnp.logical_not(is_two))
    def _():
        half, core = rows // 2, spot.tm % 2
        even_ref[pl.ds(pl.multiple_of(core * half, 8), half)] = zero_sum[...]
        even_ref[pl.ds(pl.multiple_of((1 - core) * half, 8), half)] = zero_got[...]

    weights = column_weights(spot, weights_ref, 1 - odd)
    others = column_weights(spot, weights_ref, odd)
    sides_ref[...] = beside(weights, border_mine[...] + border_got[...], odd == 1)
    step = rows // 5
    copies = []
    for n in range(5):
        here = slice(n * step, (n + 1) * step)
        own, beyond = shares(weights, others, even_ref[here], odd == 1)
        made_ref[1 - odd, here] = own + sides_ref[here] + odd_beyond[here]
        made_ref[odd, here] = odd_own[here] + beyond
        for column in range(2):
            into = out_any.at[here, column * WIDTH : (column + 1) * WIDTH]
            copies.append(pltpu.make_async_copy(made_ref.at[column, here], into, sems.at[len(copies)]))
            copies[-1].start()
    for copy in copies:
        copy.wait()


def tied(value, *others):
    return lax.optimization_barrier((value, *others))[0]


def by_ring(relation, effects, phi_one, phi_two, innov_scale):
    gens, tms = lax.axis_size("gen"), lax.axis_size("tm")
    share = gens // tms
    half = gens // 2
    rows, depth = relation.shape
    cut = depth // 256 * 128
    wide = pl.cdiv(rows, 128) * 128
    long = rows + pl.cdiv(2 * wide // 128, 8) * 8
    order = list(range(0, gens, 2)) + list(range(gens - 1, 0, -2))
    forward = [(order[p], order[(p + 1) % gens]) for p in range(gens)]
    backward = [(b, a) for a, b in forward]
    swap = [(t, t ^ 1) for t in range(tms)]
    def spot_of():
        return Spot(gens, tms)

    def ahead_of(x):
        return lax.ppermute(x, "gen", backward)

    def behind_of(x):
        return lax.ppermute(x, "gen", forward)

    def multiplied(*fars, after=(), cost=1):
        parts = [tied(x, *after) for far in fars for x in blocks[far]]
        made = call(
            products_kernel,
            [(rows, WIDTH), (4, wide)] * len(fars),
            (relation, *parts),
            [pltpu.VMEM((rows, 2 * WIDTH), jnp.float32), pltpu.VMEM((wide, WIDTH), jnp.float32)],
            flops=cost * len(fars) * KERNEL_FLOPS,
        )
        for n, far in enumerate(fars):
            products[far] = made[2 * n : 2 * n + 2]

    def over_cores(x):
        return lax.ppermute(x, "tm", swap)

    def over_y(x):
        return lax.ppermute(x, "tm", [(t, t ^ 2) for t in range(tms)])

    def in_two_steps(behind, ahead, after=(), cost=1):
        both = pltpu.VMEM((rows, 2 * WIDTH), jnp.float32)
        parts = [tied(blocks[far][1], *after) for far in (behind, ahead)]
        bottoms = call(
            functools.partial(bottom_kernel, cut),
            [(rows, WIDTH)] * 2,
            (relation, *parts),
            [both],
            flops=KERNEL_FLOPS,
        )
        made = call(
            functools.partial(top_kernel, cut),
            [(rows, WIDTH), (4, wide)] * 2,
            (relation, blocks[behind][0], blocks[ahead][0], *bottoms),
            [both, pltpu.VMEM((wide, WIDTH), jnp.float32)],
            flops=cost * KERNEL_FLOPS,
        )
        products[behind], products[ahead] = made[:2], made[2:]

    top, bottom = effects[:cut], effects[cut:]
    blocks, products = {0: (top, bottom)}, {}
    behind, ahead = blocks[0], blocks[0]
    multiplied(0)
    for n in range(1, half):
        behind_top = behind_of(behind[0] if n < 2 else tied(behind[0], *products[n - 2]))
        ahead_bottom = ahead_of(ahead[1])
        behind_bottom = behind_of(behind[1])
        ahead_top = ahead_of(ahead[0])
        behind, ahead = (behind_top, behind_bottom), (ahead_top, ahead_bottom)
        blocks[-n], blocks[n] = behind, ahead
        if n == 1:
            multiplied(-n, n)
        if n == 2:
            in_two_steps(-n, n, after=(), cost=1)
    blocks[half] = (behind_of(behind[0]), ahead_of(ahead[1]))
    two_send, two_keep = call(
        functools.partial(chip_pair_kernel, spot_of, 2),
        [(rows, WIDTH)] * 2,
        (products[2][0], products[-2][0]),
        flops=KERNEL_FLOPS // 2,
    )
    two_sum = call(sum_kernel, [(rows, WIDTH)], (two_keep, over_y(two_send)), flops=KERNEL_FLOPS // 10)[0]
    two_got = over_cores(two_sum)
    in_two_steps(1 - half, half - 1, cost=10)
    odd_fars = (-1, 3, 1, -3)
    send, keep = call(
        functools.partial(odd_kernel, spot_of, odd_fars),
        [(2 * long, WIDTH)] * 2,
        [tied(x, two_sum) for far in odd_fars for x in products[far]],
        [pltpu.VMEM((5, 4, wide), jnp.float32), pltpu.VMEM((2, long, WIDTH), jnp.float32)],
        flops=KERNEL_FLOPS // 2,
    )
    odd_send, odd_mine = call(
        functools.partial(part_sums_kernel, spot_of, odd_fars),
        [(long, WIDTH)] * 2,
        (keep, over_cores(send)),
        flops=KERNEL_FLOPS // 2,
    )
    odd_got = over_y(odd_send)
    multiplied(half, after=(odd_mine,), cost=20)
    even_fars = (0, half, 2, -2)
    border_send, border_keep = call(
        functools.partial(borders_kernel, spot_of, even_fars),
        [(4, wide)] * 2,
        [products[far][1] for far in even_fars],
        [pltpu.VMEM((5, 4, wide), jnp.float32)],
        flops=KERNEL_FLOPS // 10,
    )
    border_send, border_mine = call(
        border_sums_kernel,
        [(2, wide)] * 2,
        (border_keep, over_cores(border_send)),
        flops=KERNEL_FLOPS // 10,
    )
    border_got = over_y(border_send)
    send, keep = call(
        functools.partial(halves_kernel, spot_of, 0),
        [(rows, WIDTH)] * 2,
        [products[far][0] for far in (0, half)],
        flops=KERNEL_FLOPS // 2,
    )
    zero_send, zero_mine = call(
        half_sums_kernel,
        [(rows // 2, WIDTH)] * 2,
        (tied(keep, odd_got), over_cores(send)),
        flops=KERNEL_FLOPS // 10,
    )
    zero_sum = call(
        sum_kernel,
        [(rows // 2, WIDTH)],
        (tied(zero_mine, border_got), over_y(zero_send)),
        flops=KERNEL_FLOPS // 10,
    )[0]
    zero_got = over_cores(zero_sum)
    weights = call(weights_kernel, [(8, phi_one.shape[0])], (phi_one, phi_two, innov_scale))[0]
    odd_own, odd_beyond = call(
        functools.partial(odd_shares_kernel, spot_of),
        [(rows, WIDTH)] * 2,
        (odd_mine, tied(odd_got, zero_mine), weights),
        [pltpu.VMEM((wide, WIDTH), jnp.float32)],
        flops=KERNEL_FLOPS,
    )
    return call(
        functools.partial(last_kernel, spot_of),
        [(rows, share * WIDTH)],
        (odd_own, odd_beyond, two_sum, two_got, zero_sum, zero_got, border_mine, border_got, weights),
        [
            pltpu.VMEM((rows, WIDTH), jnp.float32),
            pltpu.VMEM((wide, WIDTH), jnp.float32),
            pltpu.VMEM((2, rows, WIDTH), jnp.float32),
            pltpu.SemaphoreType.DMA((10,)),
        ],
        into=pl.BlockSpec(memory_space=pl.ANY),
    )[0]


def extended(cells, sides, width):
    for axis, dim in sides:
        count = lax.axis_size(axis)
        ends = count - 1
        head = lax.slice_in_dim(cells, 0, width, axis=dim)
        tail = lax.slice_in_dim(cells, cells.shape[dim] - width, cells.shape[dim], axis=dim)
        cells = jnp.concatenate(
            [
                lax.ppermute(tail, axis, [(i, (i + 1) % count) for i in range(ends)]),
                cells,
                lax.ppermute(head, axis, [((i + 1) % count, i) for i in range(ends)]),
            ],
            axis=dim,
        )
    return cells


def temporal_block(widened, first_time, phi_one, phi_two, innov_scale):
    block = widened.shape[1] - 4
    zero_pair = jnp.zeros((2,), jnp.float32)
    first_pad = jnp.concatenate([phi_one, zero_pair])
    second_pad = jnp.concatenate([phi_two, zero_pair])
    scale_pad = jnp.concatenate([innov_scale, zero_pair])
    first_win = lax.dynamic_slice_in_dim(first_pad, first_time, block + 2)
    second_win = lax.dynamic_slice_in_dim(second_pad, first_time, block + 2)
    scale_win = lax.dynamic_slice_in_dim(scale_pad, first_time, block + 2)
    innov = (
        widened[:, 2:]
        - first_win[None, :] * widened[:, 1:-1]
        - second_win[None, :] * widened[:, :-2]
    )
    weighted = scale_win[None, :] * innov
    first_next = lax.dynamic_slice_in_dim(first_pad, first_time + 1, block)
    second_next = lax.dynamic_slice_in_dim(second_pad, first_time + 2, block)
    return (
        weighted[:, :block]
        - first_next[None, :] * weighted[:, 1 : block + 1]
        - second_next[None, :] * weighted[:, 2 : block + 2]
    )


def by_gather(relation, effects, phi_one, phi_two, innov_scale):
    relation_wide = relation.astype(jnp.float32)
    partial_sums = jnp.dot(
        relation_wide,
        lax.all_gather(effects, "gen", axis=1, tiled=True),
        precision=lax.Precision.HIGHEST,
        preferred_element_type=jnp.float32,
    )
    genetic = lax.psum_scatter(partial_sums, "tm", scatter_dimension=1, tiled=True)
    widened_time = extended(genetic, (("tm", 1),), 2)
    start_tm = lax.axis_index("tm") * genetic.shape[1]
    return temporal_block(widened_time, start_tm, phi_one, phi_two, innov_scale)


def on_device(relation, effects, phi_one, phi_two, innov_scale):
    gens, tms = lax.axis_size("gen"), lax.axis_size("tm")
    fits = gens == 8 and tms == 4 and effects.shape[1] == WIDTH and effects.shape[0] % 64 == 0 and relation.shape[0] % 80 == 0
    way = by_ring if fits else by_gather
    return way(relation, effects, phi_one, phi_two, innov_scale)


def solution(mesh):
    placed = (P("gen", "tm"), P("tm", "gen"), P(), P(), P())
    return jax.shard_map(
        on_device, mesh=mesh, in_specs=placed, out_specs=P("gen", "tm"), check_vma=False
    )
```

```python
import functools

import jax
import jax.numpy as jnp
from jax import lax
from jax.experimental import pallas as pl
from jax.experimental.pallas import tpu as pltpu
from jax.sharding import PartitionSpec as P

VMEM_LIMIT = 12 * 1024 * 1024
WIDTH = 128
KERNEL_FLOPS = 10**8

WHOLE = pl.BlockSpec(memory_space=pltpu.VMEM)


def call(kernel, shapes, operands, scratch=(), flops=0, into=WHOLE, last=0):
    return pl.pallas_call(
        kernel,
        out_shape=[jax.ShapeDtypeStruct(shape, jnp.float32) for shape in shapes],
        in_specs=[WHOLE] * (len(operands) - last) + [into] * last,
        input_output_aliases={len(operands) - last + n: n for n in range(last)},
        out_specs=[into] * len(shapes),
        scratch_shapes=scratch,
        compiler_params=pltpu.CompilerParams(vmem_limit_bytes=VMEM_LIMIT),
        cost_estimate=pl.CostEstimate(flops=flops, bytes_accessed=0, transcendentals=0),
    )(*operands)


def bands(phi_one, phi_two, innov_scale):
    count = phi_one.shape[1]
    row = lax.broadcasted_iota(jnp.int32, (8, count), 0)
    lane = lax.broadcasted_iota(jnp.int32, (8, count), 1)

    def rows(*values):
        out = jnp.zeros((8, count), jnp.float32)
        for n, value in enumerate(values):
            out = jnp.where(row == n, value, out)
        return out

    now = rows(phi_one, phi_two, innov_scale)
    next_1 = jnp.where(lane < count - 1, pltpu.roll(now, count - 1, 1), 0.0)
    next_2 = jnp.where(lane < count - 2, pltpu.roll(now, count - 2, 1), 0.0)
    first_0, second_0, scale_0 = (now[n : n + 1] for n in range(3))
    first_1, second_1, scale_1 = (next_1[n : n + 1] for n in range(3))
    first_2, second_2, scale_2 = (next_2[n : n + 1] for n in range(3))
    return rows(
        -scale_0 * second_0,
        first_1 * scale_1 * second_1 - scale_0 * first_0,
        scale_0 + first_1 * first_1 * scale_1 + second_2 * second_2 * scale_2,
        second_2 * scale_2 * first_2 - first_1 * scale_1,
        -second_2 * scale_2,
    )


class Spot:
    def __init__(self, gens, tms):
        self.gens, self.share, self.half = gens, gens // tms, gens // 2
        self.gen, self.tm = lax.axis_index("gen"), lax.axis_index("tm")
        self.place = self.place_of(self.gen)

    def place_of(self, gen):
        return jnp.where(gen % 2 == 0, gen // 2, self.gens - 1 - gen // 2)

    def block_at(self, far):
        p = (self.place + (far + self.gens)) % self.gens
        return jnp.where(p < self.half, 2 * p, 2 * (self.gens - 1 - p) + 1)

    def owner_of(self, far):
        return self.block_at(far) // self.share

    def keeps(self, far):
        return jnp.where(self.owner_of(far) % 2 == self.tm % 2, 1, 0)

    def border_of(self, far, fars):
        there = (2 * self.gens - 2 * self.place - far) % self.gens
        at = jnp.int32(len(fars))
        for m, other in enumerate(fars):
            if other != far:
                at = jnp.where(there == other % self.gens, m, at)
        return at


def weights_kernel(one_ref, two_ref, scale_ref, weights_ref):
    weights_ref[...] = bands(one_ref[...][None], two_ref[...][None], scale_ref[...][None])


def products_kernel(relation_ref, *refs):
    both_ref, padded_ref = refs[-2:]
    count = (len(refs) - 2) // 4
    rows = relation_ref.shape[0]
    padded_ref[...] = jnp.zeros_like(padded_ref)
    for n in range(count):
        block = jnp.concatenate([refs[2 * n][...], refs[2 * n + 1][...]], axis=0)
        high = block.astype(jnp.bfloat16)
        low = (block - high.astype(jnp.float32)).astype(jnp.bfloat16)
        both_ref[...] = jnp.dot(
            relation_ref[...],
            jnp.concatenate([high, low], axis=1),
            preferred_element_type=jnp.float32,
        )
        padded_ref[:rows] = both_ref[:, :WIDTH] + both_ref[:, WIDTH:]
        refs[2 * count + 2 * n][...] = padded_ref[:rows]
        turned = padded_ref[...].T
        edges_ref = refs[2 * count + 2 * n + 1]
        edges_ref[0:2] = turned[0:2]
        edges_ref[2:4] = turned[WIDTH - 2 :]


def bottom_kernel(cut, relation_ref, *refs):
    both_ref = refs[-1]
    count = (len(refs) - 1) // 2
    for n in range(count):
        both_ref[...] = jnp.dot(
            relation_ref[:, cut:], two_parts(refs[n][...]), preferred_element_type=jnp.float32
        )
        refs[count + n][...] = both_ref[:, :WIDTH] + both_ref[:, WIDTH:]


def top_kernel(cut, relation_ref, *refs):
    both_ref, padded_ref = refs[-2:]
    count = (len(refs) - 2) // 4
    rows = relation_ref.shape[0]
    padded_ref[...] = jnp.zeros_like(padded_ref)
    for n in range(count):
        both_ref[...] = jnp.dot(
            relation_ref[:, :cut], two_parts(refs[n][...]), preferred_element_type=jnp.float32
        )
        padded_ref[:rows] = both_ref[:, :WIDTH] + both_ref[:, WIDTH:] + refs[count + n][...]
        refs[2 * count + 2 * n][...] = padded_ref[:rows]
        turned = padded_ref[...].T
        edges_ref = refs[2 * count + 2 * n + 1]
        edges_ref[0:2] = turned[0:2]
        edges_ref[2:4] = turned[WIDTH - 2 :]


def two_parts(block):
    high = block.astype(jnp.bfloat16)
    low = (block - high.astype(jnp.float32)).astype(jnp.bfloat16)
    return jnp.concatenate([high, low], axis=1)


def odd_kernel(spot_of, fars, *refs):
    send_ref, keep_ref, edges_ref, message_ref = refs[-4:]
    spot = spot_of()
    rows, long = refs[0].shape[0], message_ref.shape[1]
    for m in range(4):
        edges_ref[m] = refs[2 * m + 1][...]
    edges_ref[4] = jnp.zeros_like(refs[1])
    for m in range(4):
        there = edges_ref[spot.border_of(fars[m], fars)]
        border = jnp.where(spot.block_at(fars[m]) % spot.share == 0, there[2:4], there[0:2])
        message_ref[m % 2, :rows] = refs[2 * m][...]
        message_ref[m % 2, rows:] = jnp.zeros((long - rows, WIDTH), jnp.float32)
        for k in range(border.shape[1] // WIDTH):
            message_ref[m % 2, rows + 2 * k : rows + 2 * k + 2] = border[:, k * WIDTH : (k + 1) * WIDTH]
        if m % 2:
            here = pl.ds(m // 2 * long, long)
            near = spot.keeps(fars[m - 1])
            keep_ref[here] = message_ref[1 - near]
            send_ref[here] = message_ref[near]


def halves_kernel(spot_of, near, near_ref, far_ref, send_ours, send_theirs, keep_ref):
    spot = spot_of()
    rows = near_ref.shape[0] // 2
    core = spot.tm % 2
    mine = spot.owner_of(near) // 2 == spot.tm // 2
    for ours in (True, False):

        @pl.when(mine == ours)
        def _():
            pairs = ((near_ref, send_ours), (far_ref, send_theirs))
            if not ours:
                pairs = ((far_ref, send_ours), (near_ref, send_theirs))
            for n, (ref, send_ref) in enumerate(pairs):
                send_ref[...] = ref[pl.ds(pl.multiple_of((1 - core) * rows, 8), rows)]
                keep_ref[pl.ds(n * rows, rows)] = ref[pl.ds(pl.multiple_of(core * rows, 8), rows)]


def half_sums_kernel(keep_ref, got_ours, got_theirs, first_ref, second_ref, mine_ref):
    rows, piece = mine_ref.shape[0], first_ref.shape[0]
    mine_ref[...] = keep_ref[:rows] + got_ours[...]
    first_ref[...] = keep_ref[rows : rows + piece] + got_theirs[:piece]
    second_ref[...] = keep_ref[rows + piece :] + got_theirs[piece:]


def pieces_sum_kernel(one_ref, first_ref, second_ref, out_ref):
    piece = first_ref.shape[0]
    out_ref[:piece] = one_ref[:piece] + first_ref[...]
    out_ref[piece:] = one_ref[piece:] + second_ref[...]


def chip_pair_kernel(spot_of, near, near_ref, far_ref, send_ref, keep_ref):
    spot = spot_of()
    mine = spot.owner_of(near) // 2 == spot.tm // 2

    @pl.when(mine)
    def _():
        keep_ref[...] = near_ref[...]
        send_ref[...] = far_ref[...]

    @pl.when(jnp.logical_not(mine))
    def _():
        keep_ref[...] = far_ref[...]
        send_ref[...] = near_ref[...]


def borders_kernel(spot_of, fars, *refs):
    send_ref, keep_ref, edges_ref = refs[-3:]
    spot = spot_of()
    for m in range(4):
        edges_ref[m] = refs[m][...]
    edges_ref[4] = jnp.zeros_like(refs[0])
    chip, core = spot.tm // 2, spot.tm % 2
    send_ref[...] = jnp.zeros_like(send_ref)
    keep_ref[...] = jnp.zeros_like(keep_ref)
    for m, far in enumerate(fars):
        owner = spot.owner_of(far)
        there = edges_ref[spot.border_of(far, fars)]
        border = jnp.where(spot.block_at(far) % spot.share == 0, there[2:4], there[0:2])
        for n in range(2):
            for out_ref, whose in ((send_ref, 1 - core), (keep_ref, core)):
                wanted = 2 * jnp.where(n == 0, chip, 1 - chip) + whose

                @pl.when(owner == wanted)
                def _():
                    out_ref[2 * n : 2 * n + 2] = border


def border_sums_kernel(keep_ref, got_ref, send_ref, mine_ref):
    mine_ref[...] = keep_ref[0:2] + got_ref[0:2]
    send_ref[...] = keep_ref[2:4] + got_ref[2:4]


def sum_kernel(one_ref, other_ref, out_ref):
    out_ref[...] = one_ref[...] + other_ref[...]


def part_sums_kernel(spot_of, fars, keep_ref, *refs):
    spot = spot_of()
    owner = jnp.where(spot.keeps(fars[0]) == 1, spot.owner_of(fars[0]), spot.owner_of(fars[1]))
    mine = jnp.where(owner // 2 == spot.tm // 2, 0, 1)
    rows = refs[-1].shape[0]
    for n in range(2):

        @pl.when(mine == n)
        def _():
            here, there = slice(n * rows, (n + 1) * rows), slice((1 - n) * rows, (2 - n) * rows)
            size = refs[0].shape[0]
            for out_ref, block in ((refs[-2], there), (refs[-1], here)):
                for m, got_ref in enumerate(refs[:-2]):
                    first, end = max(block.start, m * size), min(block.stop, (m + 1) * size)
                    if first < end:
                        out_ref[first - block.start : end - block.start] = (
                            keep_ref[first:end] + got_ref[first - m * size : end - m * size]
                        )


def row_weights(weights, far, lanes):
    return jnp.where(lanes, weights[2 + far : 3 + far], 0.0)


def beside(weights, border, left):
    span = border.shape[1]
    row = lax.broadcasted_iota(jnp.int32, (8, span), 0)
    nothing = jnp.zeros((WIDTH - 8, span), jnp.float32)
    end = WIDTH - 1
    first = weights[0:1, 0:1] * border[0:1] + weights[1:2, 0:1] * border[1:2]
    second = weights[0:1, 1:2] * border[1:2]
    above = jnp.where(row == 0, first, jnp.where(row == 1, second, 0.0))
    last = weights[3:4, end:] * border[0:1] + weights[4:5, end:] * border[1:2]
    but_last = weights[4:5, end - 1 : end] * border[0:1]
    below = jnp.where(row == 7, last, jnp.where(row == 6, but_last, 0.0))
    none = jnp.zeros_like(above)
    return jnp.concatenate(
        [jnp.where(left, above, none), nothing[: WIDTH - 16], jnp.where(left, none, below)], axis=0
    ).T


def shares(weights, other_weights, block, left):
    lane = lax.broadcasted_iota(jnp.int32, (1, WIDTH), 1)
    own = weights[2:3] * block
    beyond = 0.0
    for far in (1, 2):
        back, on = pltpu.roll(block, far, 1), pltpu.roll(block, WIDTH - far, 1)
        own += row_weights(weights, -far, lane >= far) * back
        own += row_weights(weights, far, lane < WIDTH - far) * on
        beyond += jnp.where(
            left,
            row_weights(other_weights, -far, lane < far) * back,
            row_weights(other_weights, far, lane >= WIDTH - far) * on,
        )
    return own, beyond


def odd_column(spot):
    return jnp.where((spot.place_of(spot.share * spot.tm) + spot.place) % 2 == 0, 1, 0)


def column_weights(spot, weights_ref, column):
    start = (spot.tm * 2 + column) * WIDTH
    return weights_ref[:, pl.ds(pl.multiple_of(start, WIDTH), WIDTH)]


def odd_shares_kernel(spot_of, mine_ref, got_ref, weights_ref, own_ref, beyond_ref, sides_ref):
    spot = spot_of()
    odd = odd_column(spot)
    rows, span = own_ref.shape[0], sides_ref.shape[0]
    weights = column_weights(spot, weights_ref, odd)
    others = column_weights(spot, weights_ref, 1 - odd)
    extra = mine_ref[rows:] + got_ref[rows:]
    border = jnp.concatenate([extra[2 * k : 2 * k + 2] for k in range(span // WIDTH)], axis=1)
    sides_ref[...] = beside(weights, border, odd == 0)
    step = rows // 5
    for n in range(5):
        here = slice(n * step, (n + 1) * step)
        own, beyond = shares(weights, others, mine_ref[here] + got_ref[here], odd == 0)
        own_ref[here] = own + sides_ref[here]
        beyond_ref[here] = beyond


def last_kernel(
    spot_of,
    same,
    odd_own,
    odd_beyond,
    two_sum,
    two_got,
    zero_half,
    border_mine,
    border_got,
    weights_ref,
    *refs,
):
    out_any, even_ref, sides_ref, made_ref, sems = refs[-5:]
    spot = spot_of()
    odd = odd_column(spot)
    rows = out_any.shape[0] // 2
    core = spot.tm % 2
    first = pl.multiple_of((core if same else 1 - core) * rows, 8)
    here = pl.ds(first, rows)
    is_two = (spot.owner_of(2) == spot.tm) | (spot.owner_of(-2) == spot.tm)

    @pl.when(is_two)
    def _():
        even_ref[...] = two_sum[here] + two_got[here]

    @pl.when(jnp.logical_not(is_two))
    def _():
        even_ref[...] = zero_half[...]

    weights = column_weights(spot, weights_ref, 1 - odd)
    others = column_weights(spot, weights_ref, odd)
    sides_ref[...] = beside(weights, border_mine[...] + border_got[...], odd == 1)
    pieces = 5
    step = rows // pieces
    copies = []
    for n in range(pieces):
        there = pl.ds(pl.multiple_of(first + n * step, 8), step)
        own, beyond = shares(weights, others, even_ref[n * step : (n + 1) * step], odd == 1)
        made_ref[1 - odd, n * step : (n + 1) * step] = own + sides_ref[there] + odd_beyond[there]
        made_ref[odd, n * step : (n + 1) * step] = odd_own[there] + beyond
        for column in range(2):
            into = out_any.at[there, column * WIDTH : (column + 1) * WIDTH]
            made = made_ref.at[column, n * step : (n + 1) * step]
            copies.append(pltpu.make_async_copy(made, into, sems.at[len(copies)]))
            copies[-1].start()
    for copy in copies:
        copy.wait()


def tied(value, *others):
    return lax.optimization_barrier((value, *others))[0]


def by_ring(relation, effects, phi_one, phi_two, innov_scale):
    gens, tms = lax.axis_size("gen"), lax.axis_size("tm")
    share = gens // tms
    half = gens // 2
    rows, depth = relation.shape
    cut = depth // 256 * 128
    wide = pl.cdiv(rows, 128) * 128
    long = rows + pl.cdiv(2 * wide // 128, 8) * 8
    order = list(range(0, gens, 2)) + list(range(gens - 1, 0, -2))
    forward = [(order[p], order[(p + 1) % gens]) for p in range(gens)]
    backward = [(b, a) for a, b in forward]
    swap = [(t, t ^ 1) for t in range(tms)]
    def spot_of():
        return Spot(gens, tms)

    def ahead_of(x):
        return lax.ppermute(x, "gen", backward)

    def behind_of(x):
        return lax.ppermute(x, "gen", forward)

    def multiplied(*fars, after=(), cost=1):
        parts = [tied(x, *after) for far in fars for x in blocks[far]]
        made = call(
            products_kernel,
            [(rows, WIDTH), (4, wide)] * len(fars),
            (relation, *parts),
            [pltpu.VMEM((rows, 2 * WIDTH), jnp.float32), pltpu.VMEM((wide, WIDTH), jnp.float32)],
            flops=cost * len(fars) * KERNEL_FLOPS,
        )
        for n, far in enumerate(fars):
            products[far] = made[2 * n : 2 * n + 2]

    def over_cores(x):
        return lax.ppermute(x, "tm", swap)

    def over_y(x):
        return lax.ppermute(x, "tm", [(t, t ^ 2) for t in range(tms)])

    def in_two_steps(behind, ahead, after=(), cost=1):
        both = pltpu.VMEM((rows, 2 * WIDTH), jnp.float32)
        parts = [tied(blocks[far][1], *after) for far in (behind, ahead)]
        bottoms = call(
            functools.partial(bottom_kernel, cut),
            [(rows, WIDTH)] * 2,
            (relation, *parts),
            [both],
            flops=KERNEL_FLOPS,
        )
        made = call(
            functools.partial(top_kernel, cut),
            [(rows, WIDTH), (4, wide)] * 2,
            (relation, blocks[behind][0], blocks[ahead][0], *bottoms),
            [both, pltpu.VMEM((wide, WIDTH), jnp.float32)],
            flops=cost * KERNEL_FLOPS,
        )
        products[behind], products[ahead] = made[:2], made[2:]

    top, bottom = effects[:cut], effects[cut:]
    blocks, products = {0: (top, bottom)}, {}
    behind, ahead = blocks[0], blocks[0]
    multiplied(0)
    for n in range(1, half):
        behind_top = behind_of(behind[0] if n < 2 else tied(behind[0], *products[n - 2]))
        ahead_bottom = ahead_of(ahead[1])
        behind_bottom = behind_of(behind[1])
        ahead_top = ahead_of(ahead[0])
        behind, ahead = (behind_top, behind_bottom), (ahead_top, ahead_bottom)
        blocks[-n], blocks[n] = behind, ahead
        if n == 1:
            multiplied(-n, n)
        if n == 2:
            in_two_steps(-n, n, after=(), cost=1)
    blocks[half] = (behind_of(behind[0]), ahead_of(ahead[1]))
    two_send, two_keep = call(
        functools.partial(chip_pair_kernel, spot_of, 2),
        [(rows, WIDTH)] * 2,
        (products[2][0], products[-2][0]),
        flops=KERNEL_FLOPS // 2,
    )
    two_sum = call(sum_kernel, [(rows, WIDTH)], (two_keep, over_y(two_send)), flops=KERNEL_FLOPS // 10)[0]
    two_got = over_cores(two_sum)
    in_two_steps(1 - half, half - 1, cost=10)
    odd_fars = (-1, 3, 1, -3)
    send, keep = call(
        functools.partial(odd_kernel, spot_of, odd_fars),
        [(2 * long, WIDTH)] * 2,
        [tied(x, two_sum) for far in odd_fars for x in products[far]],
        [pltpu.VMEM((5, 4, wide), jnp.float32), pltpu.VMEM((2, long, WIDTH), jnp.float32)],
        flops=KERNEL_FLOPS // 2,
    )
    odd_send, odd_mine = call(
        functools.partial(part_sums_kernel, spot_of, odd_fars),
        [(long, WIDTH)] * 2,
        (keep, *[over_cores(send[i * (2 * long // 3) : (i + 1) * (2 * long // 3)]) for i in range(3)]),
        flops=KERNEL_FLOPS // 2,
    )
    odd_got = over_y(odd_send)
    multiplied(half, after=(odd_mine,), cost=1)
    even_fars = (0, half, 2, -2)
    border_send, border_keep = call(
        functools.partial(borders_kernel, spot_of, even_fars),
        [(4, wide)] * 2,
        [products[far][1] for far in even_fars],
        [pltpu.VMEM((5, 4, wide), jnp.float32)],
        flops=KERNEL_FLOPS // 10,
    )
    border_send, border_mine = call(
        border_sums_kernel,
        [(2, wide)] * 2,
        (border_keep, over_cores(border_send)),
        flops=KERNEL_FLOPS // 10,
    )
    border_got = over_y(border_send)
    send_ours, send_theirs, keep = call(
        functools.partial(halves_kernel, spot_of, 0),
        [(rows // 2, WIDTH)] * 2 + [(rows, WIDTH)],
        [products[far][0] for far in (0, half)],
        flops=KERNEL_FLOPS // 2,
    )
    first, second, zero_mine = call(
        half_sums_kernel,
        [(rows // 4, WIDTH)] * 2 + [(rows // 2, WIDTH)],
        (keep, over_cores(send_ours), over_cores(send_theirs)),
        flops=KERNEL_FLOPS // 10,
    )
    weights = call(weights_kernel, [(8, phi_one.shape[0])], (phi_one, phi_two, innov_scale))[0]
    odd_own, odd_beyond = call(
        functools.partial(odd_shares_kernel, spot_of),
        [(rows, WIDTH)] * 2,
        (odd_mine, odd_got, weights),
        [pltpu.VMEM((wide, WIDTH), jnp.float32)],
        flops=KERNEL_FLOPS,
    )
    zero_sum = call(
        pieces_sum_kernel,
        [(rows // 2, WIDTH)],
        (tied(zero_mine, border_got, odd_own), over_y(first), over_y(second)),
        flops=KERNEL_FLOPS // 10,
    )[0]
    zero_got = over_cores(zero_sum)
    applied = ()
    for same, zero_half in ((True, zero_sum), (False, zero_got)):
        applied = call(
            functools.partial(last_kernel, spot_of, same),
            [(rows, share * WIDTH)],
            (odd_own, odd_beyond, two_sum, two_got, zero_half, border_mine, border_got, weights, *applied),
            [
                pltpu.VMEM((rows // 2, WIDTH), jnp.float32),
                pltpu.VMEM((wide, WIDTH), jnp.float32),
                pltpu.VMEM((2, rows // 2, WIDTH), jnp.float32),
                pltpu.SemaphoreType.DMA((10,)),
            ],
            into=pl.BlockSpec(memory_space=pl.ANY),
            last=len(applied),
        )
    return applied[0]


def extended(cells, sides, width):
    for axis, dim in sides:
        count = lax.axis_size(axis)
        ends = count - 1
        head = lax.slice_in_dim(cells, 0, width, axis=dim)
        tail = lax.slice_in_dim(cells, cells.shape[dim] - width, cells.shape[dim], axis=dim)
        cells = jnp.concatenate(
            [
                lax.ppermute(tail, axis, [(i, (i + 1) % count) for i in range(ends)]),
                cells,
                lax.ppermute(head, axis, [((i + 1) % count, i) for i in range(ends)]),
            ],
            axis=dim,
        )
    return cells


def temporal_block(widened, first_time, phi_one, phi_two, innov_scale):
    block = widened.shape[1] - 4
    zero_pair = jnp.zeros((2,), jnp.float32)
    first_pad = jnp.concatenate([phi_one, zero_pair])
    second_pad = jnp.concatenate([phi_two, zero_pair])
    scale_pad = jnp.concatenate([innov_scale, zero_pair])
    first_win = lax.dynamic_slice_in_dim(first_pad, first_time, block + 2)
    second_win = lax.dynamic_slice_in_dim(second_pad, first_time, block + 2)
    scale_win = lax.dynamic_slice_in_dim(scale_pad, first_time, block + 2)
    innov = (
        widened[:, 2:]
        - first_win[None, :] * widened[:, 1:-1]
        - second_win[None, :] * widened[:, :-2]
    )
    weighted = scale_win[None, :] * innov
    first_next = lax.dynamic_slice_in_dim(first_pad, first_time + 1, block)
    second_next = lax.dynamic_slice_in_dim(second_pad, first_time + 2, block)
    return (
        weighted[:, :block]
        - first_next[None, :] * weighted[:, 1 : block + 1]
        - second_next[None, :] * weighted[:, 2 : block + 2]
    )


def by_gather(relation, effects, phi_one, phi_two, innov_scale):
    relation_wide = relation.astype(jnp.float32)
    partial_sums = jnp.dot(
        relation_wide,
        lax.all_gather(effects, "gen", axis=1, tiled=True),
        precision=lax.Precision.HIGHEST,
        preferred_element_type=jnp.float32,
    )
    genetic = lax.psum_scatter(partial_sums, "tm", scatter_dimension=1, tiled=True)
    widened_time = extended(genetic, (("tm", 1),), 2)
    start_tm = lax.axis_index("tm") * genetic.shape[1]
    return temporal_block(widened_time, start_tm, phi_one, phi_two, innov_scale)


def on_device(relation, effects, phi_one, phi_two, innov_scale):
    gens, tms = lax.axis_size("gen"), lax.axis_size("tm")
    fits = gens == 8 and tms == 4 and effects.shape[1] == WIDTH and effects.shape[0] % 64 == 0 and relation.shape[0] % 160 == 0
    way = by_ring if fits else by_gather
    return way(relation, effects, phi_one, phi_two, innov_scale)


def solution(mesh):
    placed = (P("gen", "tm"), P("tm", "gen"), P(), P(), P())
    return jax.shard_map(
        on_device, mesh=mesh, in_specs=placed, out_specs=P("gen", "tm"), check_vma=False
    )
```

```python
import functools

import jax
import jax.numpy as jnp
from jax import lax
from jax.experimental import pallas as pl
from jax.experimental.pallas import tpu as pltpu
from jax.sharding import PartitionSpec as P

VMEM_LIMIT = 12 * 1024 * 1024
WIDTH = 128
KERNEL_FLOPS = 10**8

WHOLE = pl.BlockSpec(memory_space=pltpu.VMEM)


def call(kernel, shapes, operands, scratch=(), flops=0, into=WHOLE, last=0):
    return pl.pallas_call(
        kernel,
        out_shape=[jax.ShapeDtypeStruct(shape, jnp.float32) for shape in shapes],
        in_specs=[WHOLE] * (len(operands) - last) + [into] * last,
        input_output_aliases={len(operands) - last + n: n for n in range(last)},
        out_specs=[into] * len(shapes),
        scratch_shapes=scratch,
        compiler_params=pltpu.CompilerParams(vmem_limit_bytes=VMEM_LIMIT),
        cost_estimate=pl.CostEstimate(flops=flops, bytes_accessed=0, transcendentals=0),
    )(*operands)


def bands(phi_one, phi_two, innov_scale):
    count = phi_one.shape[1]
    row = lax.broadcasted_iota(jnp.int32, (8, count), 0)
    lane = lax.broadcasted_iota(jnp.int32, (8, count), 1)

    def rows(*values):
        out = jnp.zeros((8, count), jnp.float32)
        for n, value in enumerate(values):
            out = jnp.where(row == n, value, out)
        return out

    now = rows(phi_one, phi_two, innov_scale)
    next_1 = jnp.where(lane < count - 1, pltpu.roll(now, count - 1, 1), 0.0)
    next_2 = jnp.where(lane < count - 2, pltpu.roll(now, count - 2, 1), 0.0)
    first_0, second_0, scale_0 = (now[n : n + 1] for n in range(3))
    first_1, second_1, scale_1 = (next_1[n : n + 1] for n in range(3))
    first_2, second_2, scale_2 = (next_2[n : n + 1] for n in range(3))
    return rows(
        -scale_0 * second_0,
        first_1 * scale_1 * second_1 - scale_0 * first_0,
        scale_0 + first_1 * first_1 * scale_1 + second_2 * second_2 * scale_2,
        second_2 * scale_2 * first_2 - first_1 * scale_1,
        -second_2 * scale_2,
    )


class Spot:
    def __init__(self, gens, tms):
        self.gens, self.share, self.half = gens, gens // tms, gens // 2
        self.gen, self.tm = lax.axis_index("gen"), lax.axis_index("tm")
        self.place = self.place_of(self.gen)

    def place_of(self, gen):
        return jnp.where(gen % 2 == 0, gen // 2, self.gens - 1 - gen // 2)

    def block_at(self, far):
        p = (self.place + (far + self.gens)) % self.gens
        return jnp.where(p < self.half, 2 * p, 2 * (self.gens - 1 - p) + 1)

    def owner_of(self, far):
        return self.block_at(far) // self.share

    def keeps(self, far):
        return jnp.where(self.owner_of(far) % 2 == self.tm % 2, 1, 0)

    def border_of(self, far, fars):
        there = (2 * self.gens - 2 * self.place - far) % self.gens
        at = jnp.int32(len(fars))
        for m, other in enumerate(fars):
            if other != far:
                at = jnp.where(there == other % self.gens, m, at)
        return at


def weights_kernel(one_ref, two_ref, scale_ref, weights_ref):
    weights_ref[...] = bands(one_ref[...][None], two_ref[...][None], scale_ref[...][None])


def products_kernel(relation_ref, *refs):
    both_ref, padded_ref = refs[-2:]
    count = (len(refs) - 2) // 4
    rows = relation_ref.shape[0]
    padded_ref[...] = jnp.zeros_like(padded_ref)
    for n in range(count):
        block = jnp.concatenate([refs[2 * n][...], refs[2 * n + 1][...]], axis=0)
        high = block.astype(jnp.bfloat16)
        low = (block - high.astype(jnp.float32)).astype(jnp.bfloat16)
        both_ref[...] = jnp.dot(
            relation_ref[...],
            jnp.concatenate([high, low], axis=1),
            preferred_element_type=jnp.float32,
        )
        padded_ref[:rows] = both_ref[:, :WIDTH] + both_ref[:, WIDTH:]
        refs[2 * count + 2 * n][...] = padded_ref[:rows]
        turned = padded_ref[...].T
        edges_ref = refs[2 * count + 2 * n + 1]
        edges_ref[0:2] = turned[0:2]
        edges_ref[2:4] = turned[WIDTH - 2 :]


def first_part_kernel(columns, relation_ref, *refs):
    both_ref = refs[-1]
    count = (len(refs) - 1) // 2
    for n in range(count):
        both_ref[...] = jnp.dot(
            relation_ref[:, columns], two_parts(refs[n][...]), preferred_element_type=jnp.float32
        )
        refs[count + n][...] = both_ref[:, :WIDTH] + both_ref[:, WIDTH:]


def last_part_kernel(columns, relation_ref, *refs):
    both_ref, padded_ref = refs[-2:]
    count = (len(refs) - 2) // 4
    rows = relation_ref.shape[0]
    padded_ref[...] = jnp.zeros_like(padded_ref)
    for n in range(count):
        both_ref[...] = jnp.dot(
            relation_ref[:, columns], two_parts(refs[n][...]), preferred_element_type=jnp.float32
        )
        padded_ref[:rows] = both_ref[:, :WIDTH] + both_ref[:, WIDTH:] + refs[count + n][...]
        refs[2 * count + 2 * n][...] = padded_ref[:rows]
        turned = padded_ref[...].T
        edges_ref = refs[2 * count + 2 * n + 1]
        edges_ref[0:2] = turned[0:2]
        edges_ref[2:4] = turned[WIDTH - 2 :]


def two_parts(block):
    high = block.astype(jnp.bfloat16)
    low = (block - high.astype(jnp.float32)).astype(jnp.bfloat16)
    return jnp.concatenate([high, low], axis=1)


def odd_kernel(spot_of, fars, *refs):
    send_ref, keep_ref, edges_ref, message_ref = refs[-4:]
    spot = spot_of()
    rows, long = refs[0].shape[0], message_ref.shape[1]
    for m in range(4):
        edges_ref[m] = refs[2 * m + 1][...]
    edges_ref[4] = jnp.zeros_like(refs[1])
    for m in range(4):
        there = edges_ref[spot.border_of(fars[m], fars)]
        border = jnp.where(spot.block_at(fars[m]) % spot.share == 0, there[2:4], there[0:2])
        message_ref[m % 2, :rows] = refs[2 * m][...]
        message_ref[m % 2, rows:] = jnp.zeros((long - rows, WIDTH), jnp.float32)
        for k in range(border.shape[1] // WIDTH):
            message_ref[m % 2, rows + 2 * k : rows + 2 * k + 2] = border[:, k * WIDTH : (k + 1) * WIDTH]
        if m % 2:
            here = pl.ds(m // 2 * long, long)
            near = spot.keeps(fars[m - 1])
            keep_ref[here] = message_ref[1 - near]
            send_ref[here] = message_ref[near]


def halves_kernel(spot_of, near, near_ref, far_ref, send_ours, send_theirs, keep_ref):
    spot = spot_of()
    rows = near_ref.shape[0] // 2
    core = spot.tm % 2
    mine = spot.owner_of(near) // 2 == spot.tm // 2
    for ours in (True, False):

        @pl.when(mine == ours)
        def _():
            pairs = ((near_ref, send_ours), (far_ref, send_theirs))
            if not ours:
                pairs = ((far_ref, send_ours), (near_ref, send_theirs))
            for n, (ref, send_ref) in enumerate(pairs):
                send_ref[...] = ref[pl.ds(pl.multiple_of((1 - core) * rows, 8), rows)]
                keep_ref[pl.ds(n * rows, rows)] = ref[pl.ds(pl.multiple_of(core * rows, 8), rows)]


def half_sums_kernel(keep_ref, got_ours, got_theirs, first_ref, second_ref, mine_ref):
    rows, piece = mine_ref.shape[0], first_ref.shape[0]
    mine_ref[...] = keep_ref[:rows] + got_ours[...]
    first_ref[...] = keep_ref[rows : rows + piece] + got_theirs[:piece]
    second_ref[...] = keep_ref[rows + piece :] + got_theirs[piece:]


def pieces_sum_kernel(one_ref, first_ref, second_ref, out_ref):
    piece = first_ref.shape[0]
    out_ref[:piece] = one_ref[:piece] + first_ref[...]
    out_ref[piece:] = one_ref[piece:] + second_ref[...]


def chip_pair_kernel(spot_of, near, near_ref, far_ref, send_ref, keep_ref):
    spot = spot_of()
    mine = spot.owner_of(near) // 2 == spot.tm // 2

    @pl.when(mine)
    def _():
        keep_ref[...] = near_ref[...]
        send_ref[...] = far_ref[...]

    @pl.when(jnp.logical_not(mine))
    def _():
        keep_ref[...] = far_ref[...]
        send_ref[...] = near_ref[...]


def borders_kernel(spot_of, fars, *refs):
    send_ref, keep_ref, edges_ref = refs[-3:]
    spot = spot_of()
    for m in range(4):
        edges_ref[m] = refs[m][...]
    edges_ref[4] = jnp.zeros_like(refs[0])
    chip, core = spot.tm // 2, spot.tm % 2
    send_ref[...] = jnp.zeros_like(send_ref)
    keep_ref[...] = jnp.zeros_like(keep_ref)
    for m, far in enumerate(fars):
        owner = spot.owner_of(far)
        there = edges_ref[spot.border_of(far, fars)]
        border = jnp.where(spot.block_at(far) % spot.share == 0, there[2:4], there[0:2])
        for n in range(2):
            for out_ref, whose in ((send_ref, 1 - core), (keep_ref, core)):
                wanted = 2 * jnp.where(n == 0, chip, 1 - chip) + whose

                @pl.when(owner == wanted)
                def _():
                    out_ref[2 * n : 2 * n + 2] = border


def border_sums_kernel(keep_ref, got_ref, send_ref, mine_ref):
    mine_ref[...] = keep_ref[0:2] + got_ref[0:2]
    send_ref[...] = keep_ref[2:4] + got_ref[2:4]


def sum_kernel(one_ref, other_ref, out_ref):
    out_ref[...] = one_ref[...] + other_ref[...]


def part_sums_kernel(spot_of, fars, keep_ref, *refs):
    spot = spot_of()
    owner = jnp.where(spot.keeps(fars[0]) == 1, spot.owner_of(fars[0]), spot.owner_of(fars[1]))
    mine = jnp.where(owner // 2 == spot.tm // 2, 0, 1)
    rows = refs[-1].shape[0]
    for n in range(2):

        @pl.when(mine == n)
        def _():
            here, there = slice(n * rows, (n + 1) * rows), slice((1 - n) * rows, (2 - n) * rows)
            size = refs[0].shape[0]
            for out_ref, block in ((refs[-2], there), (refs[-1], here)):
                for m, got_ref in enumerate(refs[:-2]):
                    first, end = max(block.start, m * size), min(block.stop, (m + 1) * size)
                    if first < end:
                        out_ref[first - block.start : end - block.start] = (
                            keep_ref[first:end] + got_ref[first - m * size : end - m * size]
                        )


def row_weights(weights, far, lanes):
    return jnp.where(lanes, weights[2 + far : 3 + far], 0.0)


def beside(weights, border, left):
    span = border.shape[1]
    row = lax.broadcasted_iota(jnp.int32, (8, span), 0)
    nothing = jnp.zeros((WIDTH - 8, span), jnp.float32)
    end = WIDTH - 1
    first = weights[0:1, 0:1] * border[0:1] + weights[1:2, 0:1] * border[1:2]
    second = weights[0:1, 1:2] * border[1:2]
    above = jnp.where(row == 0, first, jnp.where(row == 1, second, 0.0))
    last = weights[3:4, end:] * border[0:1] + weights[4:5, end:] * border[1:2]
    but_last = weights[4:5, end - 1 : end] * border[0:1]
    below = jnp.where(row == 7, last, jnp.where(row == 6, but_last, 0.0))
    none = jnp.zeros_like(above)
    return jnp.concatenate(
        [jnp.where(left, above, none), nothing[: WIDTH - 16], jnp.where(left, none, below)], axis=0
    ).T


def shares(weights, other_weights, block, left):
    lane = lax.broadcasted_iota(jnp.int32, (1, WIDTH), 1)
    own = weights[2:3] * block
    beyond = 0.0
    for far in (1, 2):
        back, on = pltpu.roll(block, far, 1), pltpu.roll(block, WIDTH - far, 1)
        own += row_weights(weights, -far, lane >= far) * back
        own += row_weights(weights, far, lane < WIDTH - far) * on
        beyond += jnp.where(
            left,
            row_weights(other_weights, -far, lane < far) * back,
            row_weights(other_weights, far, lane >= WIDTH - far) * on,
        )
    return own, beyond


def odd_column(spot):
    return jnp.where((spot.place_of(spot.share * spot.tm) + spot.place) % 2 == 0, 1, 0)


def column_weights(spot, weights_ref, column):
    start = (spot.tm * 2 + column) * WIDTH
    return weights_ref[:, pl.ds(pl.multiple_of(start, WIDTH), WIDTH)]


def odd_shares_kernel(spot_of, mine_ref, got_ref, weights_ref, own_ref, beyond_ref, sides_ref):
    spot = spot_of()
    odd = odd_column(spot)
    rows, span = own_ref.shape[0], sides_ref.shape[0]
    weights = column_weights(spot, weights_ref, odd)
    others = column_weights(spot, weights_ref, 1 - odd)
    extra = mine_ref[rows:] + got_ref[rows:]
    border = jnp.concatenate([extra[2 * k : 2 * k + 2] for k in range(span // WIDTH)], axis=1)
    sides_ref[...] = beside(weights, border, odd == 0)
    step = rows // 5
    for n in range(5):
        here = slice(n * step, (n + 1) * step)
        own, beyond = shares(weights, others, mine_ref[here] + got_ref[here], odd == 0)
        own_ref[here] = own + sides_ref[here]
        beyond_ref[here] = beyond


def last_kernel(
    spot_of,
    same,
    odd_own,
    odd_beyond,
    two_sum,
    two_got,
    zero_half,
    border_mine,
    border_got,
    weights_ref,
    *refs,
):
    out_any, even_ref, sides_ref, made_ref, sems = refs[-5:]
    spot = spot_of()
    odd = odd_column(spot)
    rows = out_any.shape[0] // 2
    core = spot.tm % 2
    first = pl.multiple_of((core if same else 1 - core) * rows, 8)
    here = pl.ds(first, rows)
    is_two = (spot.owner_of(2) == spot.tm) | (spot.owner_of(-2) == spot.tm)

    @pl.when(is_two)
    def _():
        even_ref[...] = two_sum[here] + two_got[here]

    @pl.when(jnp.logical_not(is_two))
    def _():
        even_ref[...] = zero_half[...]

    weights = column_weights(spot, weights_ref, 1 - odd)
    others = column_weights(spot, weights_ref, odd)
    sides_ref[...] = beside(weights, border_mine[...] + border_got[...], odd == 1)
    pieces = 5
    step = rows // pieces
    copies = []
    for n in range(pieces):
        there = pl.ds(pl.multiple_of(first + n * step, 8), step)
        own, beyond = shares(weights, others, even_ref[n * step : (n + 1) * step], odd == 1)
        made_ref[1 - odd, n * step : (n + 1) * step] = own + sides_ref[there] + odd_beyond[there]
        made_ref[odd, n * step : (n + 1) * step] = odd_own[there] + beyond
        for column in range(2):
            into = out_any.at[there, column * WIDTH : (column + 1) * WIDTH]
            made = made_ref.at[column, n * step : (n + 1) * step]
            copies.append(pltpu.make_async_copy(made, into, sems.at[len(copies)]))
            copies[-1].start()
    for copy in copies:
        copy.wait()


def tied(value, *others):
    return lax.optimization_barrier((value, *others))[0]


def by_ring(relation, effects, phi_one, phi_two, innov_scale):
    gens, tms = lax.axis_size("gen"), lax.axis_size("tm")
    share = gens // tms
    half = gens // 2
    rows, depth = relation.shape
    cut = depth // 256 * 128
    wide = pl.cdiv(rows, 128) * 128
    long = rows + pl.cdiv(2 * wide // 128, 8) * 8
    order = list(range(0, gens, 2)) + list(range(gens - 1, 0, -2))
    forward = [(order[p], order[(p + 1) % gens]) for p in range(gens)]
    backward = [(b, a) for a, b in forward]
    swap = [(t, t ^ 1) for t in range(tms)]
    def spot_of():
        return Spot(gens, tms)

    def ahead_of(x):
        return lax.ppermute(x, "gen", backward)

    def behind_of(x):
        return lax.ppermute(x, "gen", forward)

    def multiplied(*fars, after=(), cost=1):
        parts = [tied(x, *after) for far in fars for x in blocks[far]]
        made = call(
            products_kernel,
            [(rows, WIDTH), (4, wide)] * len(fars),
            (relation, *parts),
            [pltpu.VMEM((rows, 2 * WIDTH), jnp.float32), pltpu.VMEM((wide, WIDTH), jnp.float32)],
            flops=cost * len(fars) * KERNEL_FLOPS,
        )
        for n, far in enumerate(fars):
            products[far] = made[2 * n : 2 * n + 2]

    def over_cores(x):
        return lax.ppermute(x, "tm", swap)

    def over_y(x):
        return lax.ppermute(x, "tm", [(t, t ^ 2) for t in range(tms)])

    def in_two_steps(behind, ahead, after=(), cost=1, between=lambda *made: None):
        both = pltpu.VMEM((rows, 2 * WIDTH), jnp.float32)
        parts = [tied(blocks[far][1], *after) for far in (behind, ahead)]
        bottoms = call(
            functools.partial(first_part_kernel, slice(cut, depth)),
            [(rows, WIDTH)] * 2,
            (relation, *parts),
            [both],
            flops=KERNEL_FLOPS,
        )
        between(*bottoms)
        made = call(
            functools.partial(last_part_kernel, slice(0, cut)),
            [(rows, WIDTH), (4, wide)] * 2,
            (relation, blocks[behind][0], blocks[ahead][0], *bottoms),
            [both, pltpu.VMEM((wide, WIDTH), jnp.float32)],
            flops=cost * KERNEL_FLOPS,
        )
        products[behind], products[ahead] = made[:2], made[2:]

    top, bottom = effects[:cut], effects[cut:]
    blocks, products = {0: (top, bottom)}, {}
    behind, ahead = blocks[0], blocks[0]
    multiplied(0)
    for n in range(1, half):
        behind_top = behind_of(behind[0] if n < 2 else tied(behind[0], *products[n - 2]))
        ahead_bottom = ahead_of(ahead[1])
        behind_bottom = behind_of(behind[1])
        ahead_top = ahead_of(ahead[0])
        behind, ahead = (behind_top, behind_bottom), (ahead_top, ahead_bottom)
        blocks[-n], blocks[n] = behind, ahead
        if n == 1:
            multiplied(-n, n)
        if n == 2:
            in_two_steps(-n, n, after=(), cost=1)
    two_send, two_keep = call(
        functools.partial(chip_pair_kernel, spot_of, 2),
        [(rows, WIDTH)] * 2,
        (products[2][0], products[-2][0]),
        flops=KERNEL_FLOPS // 2,
    )
    two_sum = call(sum_kernel, [(rows, WIDTH)], (two_keep, over_y(two_send)), flops=KERNEL_FLOPS // 10)[0]
    two_got = over_cores(two_sum)
    def last_step(*made):
        blocks[half] = (behind_of(tied(behind[0], *made)), ahead_of(ahead[1]))

    in_two_steps(1 - half, half - 1, cost=10, between=last_step)
    odd_fars = (-1, 3, 1, -3)
    send, keep = call(
        functools.partial(odd_kernel, spot_of, odd_fars),
        [(2 * long, WIDTH)] * 2,
        [tied(x, two_sum) for far in odd_fars for x in products[far]],
        [pltpu.VMEM((5, 4, wide), jnp.float32), pltpu.VMEM((2, long, WIDTH), jnp.float32)],
        flops=KERNEL_FLOPS // 2,
    )
    odd_send, odd_mine = call(
        functools.partial(part_sums_kernel, spot_of, odd_fars),
        [(long, WIDTH)] * 2,
        (keep, *[over_cores(send[i * (2 * long // 3) : (i + 1) * (2 * long // 3)]) for i in range(3)]),
        flops=KERNEL_FLOPS // 2,
    )
    odd_got = over_y(odd_send)
    both = pltpu.VMEM((rows, 2 * WIDTH), jnp.float32)
    top_product = call(
        functools.partial(first_part_kernel, slice(0, cut)),
        [(rows, WIDTH)],
        (relation, tied(blocks[half][0], odd_mine)),
        [both],
        flops=1 * KERNEL_FLOPS,
    )[0]
    products[half] = call(
        functools.partial(last_part_kernel, slice(cut, depth)),
        [(rows, WIDTH), (4, wide)],
        (relation, tied(blocks[half][1], odd_mine), top_product),
        [both, pltpu.VMEM((wide, WIDTH), jnp.float32)],
        flops=10 * KERNEL_FLOPS,
    )
    even_fars = (0, half, 2, -2)
    border_send, border_keep = call(
        functools.partial(borders_kernel, spot_of, even_fars),
        [(4, wide)] * 2,
        [products[far][1] for far in even_fars],
        [pltpu.VMEM((5, 4, wide), jnp.float32)],
        flops=KERNEL_FLOPS // 10,
    )
    border_send, border_mine = call(
        border_sums_kernel,
        [(2, wide)] * 2,
        (border_keep, over_cores(border_send)),
        flops=KERNEL_FLOPS // 10,
    )
    border_got = over_y(border_send)
    send_ours, send_theirs, keep = call(
        functools.partial(halves_kernel, spot_of, 0),
        [(rows // 2, WIDTH)] * 2 + [(rows, WIDTH)],
        [products[far][0] for far in (0, half)],
        flops=KERNEL_FLOPS // 2,
    )
    first, second, zero_mine = call(
        half_sums_kernel,
        [(rows // 4, WIDTH)] * 2 + [(rows // 2, WIDTH)],
        (keep, over_cores(send_ours), over_cores(send_theirs)),
        flops=KERNEL_FLOPS // 10,
    )
    weights = call(weights_kernel, [(8, phi_one.shape[0])], (phi_one, phi_two, innov_scale))[0]
    odd_own, odd_beyond = call(
        functools.partial(odd_shares_kernel, spot_of),
        [(rows, WIDTH)] * 2,
        (odd_mine, odd_got, weights),
        [pltpu.VMEM((wide, WIDTH), jnp.float32)],
        flops=KERNEL_FLOPS,
    )
    zero_sum = call(
        pieces_sum_kernel,
        [(rows // 2, WIDTH)],
        (tied(zero_mine, border_got, odd_own), over_y(first), over_y(second)),
        flops=KERNEL_FLOPS // 10,
    )[0]
    zero_got = over_cores(zero_sum)
    applied = ()
    for same, zero_half in ((True, zero_sum), (False, zero_got)):
        applied = call(
            functools.partial(last_kernel, spot_of, same),
            [(rows, share * WIDTH)],
            (odd_own, odd_beyond, two_sum, two_got, zero_half, border_mine, border_got, weights, *applied),
            [
                pltpu.VMEM((rows // 2, WIDTH), jnp.float32),
                pltpu.VMEM((wide, WIDTH), jnp.float32),
                pltpu.VMEM((2, rows // 2, WIDTH), jnp.float32),
                pltpu.SemaphoreType.DMA((10,)),
            ],
            into=pl.BlockSpec(memory_space=pl.ANY),
            last=len(applied),
        )
    return applied[0]


def extended(cells, sides, width):
    for axis, dim in sides:
        count = lax.axis_size(axis)
        ends = count - 1
        head = lax.slice_in_dim(cells, 0, width, axis=dim)
        tail = lax.slice_in_dim(cells, cells.shape[dim] - width, cells.shape[dim], axis=dim)
        cells = jnp.concatenate(
            [
                lax.ppermute(tail, axis, [(i, (i + 1) % count) for i in range(ends)]),
                cells,
                lax.ppermute(head, axis, [((i + 1) % count, i) for i in range(ends)]),
            ],
            axis=dim,
        )
    return cells


def temporal_block(widened, first_time, phi_one, phi_two, innov_scale):
    block = widened.shape[1] - 4
    zero_pair = jnp.zeros((2,), jnp.float32)
    first_pad = jnp.concatenate([phi_one, zero_pair])
    second_pad = jnp.concatenate([phi_two, zero_pair])
    scale_pad = jnp.concatenate([innov_scale, zero_pair])
    first_win = lax.dynamic_slice_in_dim(first_pad, first_time, block + 2)
    second_win = lax.dynamic_slice_in_dim(second_pad, first_time, block + 2)
    scale_win = lax.dynamic_slice_in_dim(scale_pad, first_time, block + 2)
    innov = (
        widened[:, 2:]
        - first_win[None, :] * widened[:, 1:-1]
        - second_win[None, :] * widened[:, :-2]
    )
    weighted = scale_win[None, :] * innov
    first_next = lax.dynamic_slice_in_dim(first_pad, first_time + 1, block)
    second_next = lax.dynamic_slice_in_dim(second_pad, first_time + 2, block)
    return (
        weighted[:, :block]
        - first_next[None, :] * weighted[:, 1 : block + 1]
        - second_next[None, :] * weighted[:, 2 : block + 2]
    )


def by_gather(relation, effects, phi_one, phi_two, innov_scale):
    relation_wide = relation.astype(jnp.float32)
    partial_sums = jnp.dot(
        relation_wide,
        lax.all_gather(effects, "gen", axis=1, tiled=True),
        precision=lax.Precision.HIGHEST,
        preferred_element_type=jnp.float32,
    )
    genetic = lax.psum_scatter(partial_sums, "tm", scatter_dimension=1, tiled=True)
    widened_time = extended(genetic, (("tm", 1),), 2)
    start_tm = lax.axis_index("tm") * genetic.shape[1]
    return temporal_block(widened_time, start_tm, phi_one, phi_two, innov_scale)


def on_device(relation, effects, phi_one, phi_two, innov_scale):
    gens, tms = lax.axis_size("gen"), lax.axis_size("tm")
    fits = gens == 8 and tms == 4 and effects.shape[1] == WIDTH and effects.shape[0] % 64 == 0 and relation.shape[0] % 160 == 0
    way = by_ring if fits else by_gather
    return way(relation, effects, phi_one, phi_two, innov_scale)


def solution(mesh):
    placed = (P("gen", "tm"), P("tm", "gen"), P(), P(), P())
    return jax.shard_map(
        on_device, mesh=mesh, in_specs=placed, out_specs=P("gen", "tm"), check_vma=False
    )
```

```python
import functools

import jax
import jax.numpy as jnp
from jax import lax
from jax.experimental import pallas as pl
from jax.experimental.pallas import tpu as pltpu
from jax.sharding import PartitionSpec as P

VMEM_LIMIT = 12 * 1024 * 1024
WIDTH = 128
KERNEL_FLOPS = 10**8

WHOLE = pl.BlockSpec(memory_space=pltpu.VMEM)


def call(kernel, shapes, operands, scratch=(), flops=0, into=None, last=0):
    return pl.pallas_call(
        kernel,
        out_shape=[jax.ShapeDtypeStruct(shape, jnp.float32) for shape in shapes],
        in_specs=[WHOLE] * (len(operands) - last) + (into[:last] if last else []),
        input_output_aliases={len(operands) - last + n: n for n in range(last)},
        out_specs=into or [WHOLE] * len(shapes),
        scratch_shapes=scratch,
        compiler_params=pltpu.CompilerParams(vmem_limit_bytes=VMEM_LIMIT),
        cost_estimate=pl.CostEstimate(flops=flops, bytes_accessed=0, transcendentals=0),
    )(*operands)


def bands(phi_one, phi_two, innov_scale):
    count = phi_one.shape[1]
    row = lax.broadcasted_iota(jnp.int32, (8, count), 0)
    lane = lax.broadcasted_iota(jnp.int32, (8, count), 1)

    def rows(*values):
        out = jnp.zeros((8, count), jnp.float32)
        for n, value in enumerate(values):
            out = jnp.where(row == n, value, out)
        return out

    now = rows(phi_one, phi_two, innov_scale)
    next_1 = jnp.where(lane < count - 1, pltpu.roll(now, count - 1, 1), 0.0)
    next_2 = jnp.where(lane < count - 2, pltpu.roll(now, count - 2, 1), 0.0)
    first_0, second_0, scale_0 = (now[n : n + 1] for n in range(3))
    first_1, second_1, scale_1 = (next_1[n : n + 1] for n in range(3))
    first_2, second_2, scale_2 = (next_2[n : n + 1] for n in range(3))
    return rows(
        -scale_0 * second_0,
        first_1 * scale_1 * second_1 - scale_0 * first_0,
        scale_0 + first_1 * first_1 * scale_1 + second_2 * second_2 * scale_2,
        second_2 * scale_2 * first_2 - first_1 * scale_1,
        -second_2 * scale_2,
    )


class Spot:
    def __init__(self, gens, tms):
        self.gens, self.share, self.half = gens, gens // tms, gens // 2
        self.gen, self.tm = lax.axis_index("gen"), lax.axis_index("tm")
        self.place = self.place_of(self.gen)

    def place_of(self, gen):
        return jnp.where(gen % 2 == 0, gen // 2, self.gens - 1 - gen // 2)

    def block_at(self, far):
        p = (self.place + (far + self.gens)) % self.gens
        return jnp.where(p < self.half, 2 * p, 2 * (self.gens - 1 - p) + 1)

    def owner_of(self, far):
        return self.block_at(far) // self.share

    def keeps(self, far):
        return jnp.where(self.owner_of(far) % 2 == self.tm % 2, 1, 0)

    def border_of(self, far, fars):
        there = (2 * self.gens - 2 * self.place - far) % self.gens
        at = jnp.int32(len(fars))
        for m, other in enumerate(fars):
            if other != far:
                at = jnp.where(there == other % self.gens, m, at)
        return at


def weights_kernel(one_ref, two_ref, scale_ref, weights_ref):
    weights_ref[...] = bands(one_ref[...][None], two_ref[...][None], scale_ref[...][None])


def products_kernel(relation_ref, *refs):
    both_ref, padded_ref = refs[-2:]
    count = (len(refs) - 2) // 4
    rows = relation_ref.shape[0]
    padded_ref[...] = jnp.zeros_like(padded_ref)
    for n in range(count):
        block = jnp.concatenate([refs[2 * n][...], refs[2 * n + 1][...]], axis=0)
        high = block.astype(jnp.bfloat16)
        low = (block - high.astype(jnp.float32)).astype(jnp.bfloat16)
        both_ref[...] = jnp.dot(
            relation_ref[...],
            jnp.concatenate([high, low], axis=1),
            preferred_element_type=jnp.float32,
        )
        padded_ref[:rows] = both_ref[:, :WIDTH] + both_ref[:, WIDTH:]
        refs[2 * count + 2 * n][...] = padded_ref[:rows]
        turned = padded_ref[...].T
        edges_ref = refs[2 * count + 2 * n + 1]
        edges_ref[0:2] = turned[0:2]
        edges_ref[2:4] = turned[WIDTH - 2 :]


def first_part_kernel(columns, relation_ref, *refs):
    both_ref = refs[-1]
    count = (len(refs) - 1) // 2
    for n in range(count):
        both_ref[...] = jnp.dot(
            relation_ref[:, columns], two_parts(refs[n][...]), preferred_element_type=jnp.float32
        )
        refs[count + n][...] = both_ref[:, :WIDTH] + both_ref[:, WIDTH:]


def last_part_kernel(columns, relation_ref, *refs):
    both_ref, padded_ref = refs[-2:]
    count = (len(refs) - 2) // 4
    rows = relation_ref.shape[0]
    padded_ref[...] = jnp.zeros_like(padded_ref)
    for n in range(count):
        both_ref[...] = jnp.dot(
            relation_ref[:, columns], two_parts(refs[n][...]), preferred_element_type=jnp.float32
        )
        padded_ref[:rows] = both_ref[:, :WIDTH] + both_ref[:, WIDTH:] + refs[count + n][...]
        refs[2 * count + 2 * n][...] = padded_ref[:rows]
        turned = padded_ref[...].T
        edges_ref = refs[2 * count + 2 * n + 1]
        edges_ref[0:2] = turned[0:2]
        edges_ref[2:4] = turned[WIDTH - 2 :]


def two_parts(block):
    high = block.astype(jnp.bfloat16)
    low = (block - high.astype(jnp.float32)).astype(jnp.bfloat16)
    return jnp.concatenate([high, low], axis=1)


def odd_kernel(spot_of, fars, *refs):
    send_ref, keep_ref, edges_ref, message_ref = refs[-4:]
    spot = spot_of()
    rows, long = refs[0].shape[0], message_ref.shape[1]
    for m in range(4):
        edges_ref[m] = refs[2 * m + 1][...]
    edges_ref[4] = jnp.zeros_like(refs[1])
    for m in range(4):
        there = edges_ref[spot.border_of(fars[m], fars)]
        border = jnp.where(spot.block_at(fars[m]) % spot.share == 0, there[2:4], there[0:2])
        message_ref[m % 2, :rows] = refs[2 * m][...]
        message_ref[m % 2, rows:] = jnp.zeros((long - rows, WIDTH), jnp.float32)
        for k in range(border.shape[1] // WIDTH):
            message_ref[m % 2, rows + 2 * k : rows + 2 * k + 2] = border[:, k * WIDTH : (k + 1) * WIDTH]
        if m % 2:
            here = pl.ds(m // 2 * long, long)
            near = spot.keeps(fars[m - 1])
            keep_ref[here] = message_ref[1 - near]
            send_ref[here] = message_ref[near]


def halves_kernel(spot_of, near, near_ref, far_ref, send_ours, send_theirs, keep_ref):
    spot = spot_of()
    rows = near_ref.shape[0] // 2
    core = spot.tm % 2
    mine = spot.owner_of(near) // 2 == spot.tm // 2
    for ours in (True, False):

        @pl.when(mine == ours)
        def _():
            pairs = ((near_ref, send_ours), (far_ref, send_theirs))
            if not ours:
                pairs = ((far_ref, send_ours), (near_ref, send_theirs))
            for n, (ref, send_ref) in enumerate(pairs):
                send_ref[...] = ref[pl.ds(pl.multiple_of((1 - core) * rows, 8), rows)]
                keep_ref[pl.ds(n * rows, rows)] = ref[pl.ds(pl.multiple_of(core * rows, 8), rows)]


def half_sums_kernel(keep_ref, got_ours, got_theirs, send_ref, mine_ref):
    rows = mine_ref.shape[0]
    mine_ref[...] = keep_ref[:rows] + got_ours[...]
    send_ref[...] = keep_ref[rows:] + got_theirs[...]


def chip_pair_kernel(spot_of, near, near_ref, far_ref, send_ref, keep_ref):
    spot = spot_of()
    mine = spot.owner_of(near) // 2 == spot.tm // 2

    @pl.when(mine)
    def _():
        keep_ref[...] = near_ref[...]
        send_ref[...] = far_ref[...]

    @pl.when(jnp.logical_not(mine))
    def _():
        keep_ref[...] = far_ref[...]
        send_ref[...] = near_ref[...]


def borders_kernel(spot_of, fars, *refs):
    send_ref, keep_ref, edges_ref = refs[-3:]
    spot = spot_of()
    for m in range(4):
        edges_ref[m] = refs[m][...]
    edges_ref[4] = jnp.zeros_like(refs[0])
    chip, core = spot.tm // 2, spot.tm % 2
    send_ref[...] = jnp.zeros_like(send_ref)
    keep_ref[...] = jnp.zeros_like(keep_ref)
    for m, far in enumerate(fars):
        owner = spot.owner_of(far)
        there = edges_ref[spot.border_of(far, fars)]
        border = jnp.where(spot.block_at(far) % spot.share == 0, there[2:4], there[0:2])
        for n in range(2):
            for out_ref, whose in ((send_ref, 1 - core), (keep_ref, core)):
                wanted = 2 * jnp.where(n == 0, chip, 1 - chip) + whose

                @pl.when(owner == wanted)
                def _():
                    out_ref[2 * n : 2 * n + 2] = border


def border_sums_kernel(keep_ref, got_ref, send_ref, mine_ref):
    mine_ref[...] = keep_ref[0:2] + got_ref[0:2]
    send_ref[...] = keep_ref[2:4] + got_ref[2:4]


def sum_kernel(one_ref, other_ref, out_ref):
    out_ref[...] = one_ref[...] + other_ref[...]


def part_sums_kernel(spot_of, fars, keep_ref, *refs):
    spot = spot_of()
    owner = jnp.where(spot.keeps(fars[0]) == 1, spot.owner_of(fars[0]), spot.owner_of(fars[1]))
    mine = jnp.where(owner // 2 == spot.tm // 2, 0, 1)
    rows = refs[-1].shape[0]
    for n in range(2):

        @pl.when(mine == n)
        def _():
            here, there = slice(n * rows, (n + 1) * rows), slice((1 - n) * rows, (2 - n) * rows)
            size = refs[0].shape[0]
            for out_ref, block in ((refs[-2], there), (refs[-1], here)):
                for m, got_ref in enumerate(refs[:-2]):
                    first, end = max(block.start, m * size), min(block.stop, (m + 1) * size)
                    if first < end:
                        out_ref[first - block.start : end - block.start] = (
                            keep_ref[first:end] + got_ref[first - m * size : end - m * size]
                        )


def row_weights(weights, far, lanes):
    return jnp.where(lanes, weights[2 + far : 3 + far], 0.0)


def beside(weights, border, left):
    span = border.shape[1]
    row = lax.broadcasted_iota(jnp.int32, (8, span), 0)
    nothing = jnp.zeros((WIDTH - 8, span), jnp.float32)
    end = WIDTH - 1
    first = weights[0:1, 0:1] * border[0:1] + weights[1:2, 0:1] * border[1:2]
    second = weights[0:1, 1:2] * border[1:2]
    above = jnp.where(row == 0, first, jnp.where(row == 1, second, 0.0))
    last = weights[3:4, end:] * border[0:1] + weights[4:5, end:] * border[1:2]
    but_last = weights[4:5, end - 1 : end] * border[0:1]
    below = jnp.where(row == 7, last, jnp.where(row == 6, but_last, 0.0))
    none = jnp.zeros_like(above)
    return jnp.concatenate(
        [jnp.where(left, above, none), nothing[: WIDTH - 16], jnp.where(left, none, below)], axis=0
    ).T


def shares(weights, other_weights, block, left):
    lane = lax.broadcasted_iota(jnp.int32, (1, WIDTH), 1)
    own = weights[2:3] * block
    beyond = 0.0
    for far in (1, 2):
        back, on = pltpu.roll(block, far, 1), pltpu.roll(block, WIDTH - far, 1)
        own += row_weights(weights, -far, lane >= far) * back
        own += row_weights(weights, far, lane < WIDTH - far) * on
        beyond += jnp.where(
            left,
            row_weights(other_weights, -far, lane < far) * back,
            row_weights(other_weights, far, lane >= WIDTH - far) * on,
        )
    return own, beyond


def odd_column(spot):
    return jnp.where((spot.place_of(spot.share * spot.tm) + spot.place) % 2 == 0, 1, 0)


def column_weights(spot, weights_ref, column):
    start = (spot.tm * 2 + column) * WIDTH
    return weights_ref[:, pl.ds(pl.multiple_of(start, WIDTH), WIDTH)]


def odd_shares_kernel(spot_of, mine_ref, got_ref, weights_ref, own_ref, beyond_ref, sides_ref):
    spot = spot_of()
    odd = odd_column(spot)
    rows, span = own_ref.shape[0], sides_ref.shape[0]
    weights = column_weights(spot, weights_ref, odd)
    others = column_weights(spot, weights_ref, 1 - odd)
    extra = mine_ref[rows:] + got_ref[rows:]
    border = jnp.concatenate([extra[2 * k : 2 * k + 2] for k in range(span // WIDTH)], axis=1)
    sides_ref[...] = beside(weights, border, odd == 0)
    step = rows // 5
    for n in range(5):
        here = slice(n * step, (n + 1) * step)
        own, beyond = shares(weights, others, mine_ref[here] + got_ref[here], odd == 0)
        own_ref[here] = own + sides_ref[here]
        beyond_ref[here] = beyond


def last_kernel(
    spot_of,
    same,
    odd_own,
    odd_beyond,
    two_sum,
    two_got,
    zero_half,
    border_mine,
    border_got,
    weights_ref,
    *refs,
):
    out_any, sides_ref, even_ref, made_ref, sems = refs[-5:] if same else (refs[-4], refs[0], *refs[-3:])
    spot = spot_of()
    odd = odd_column(spot)
    rows = out_any.shape[0] // 2
    core = spot.tm % 2
    first = pl.multiple_of((core if same else 1 - core) * rows, 8)
    here = pl.ds(first, rows)
    is_two = (spot.owner_of(2) == spot.tm) | (spot.owner_of(-2) == spot.tm)

    @pl.when(is_two)
    def _():
        even_ref[...] = two_sum[here] + two_got[here]

    @pl.when(jnp.logical_not(is_two))
    def _():
        even_ref[...] = zero_half[...]

    weights = column_weights(spot, weights_ref, 1 - odd)
    others = column_weights(spot, weights_ref, odd)
    if same:
        sides_ref[...] = beside(weights, border_mine[...] + border_got[...], odd == 1)
    pieces = 5
    step = rows // pieces
    copies = []
    for n in range(pieces):
        there = pl.ds(pl.multiple_of(first + n * step, 8), step)
        own, beyond = shares(weights, others, even_ref[n * step : (n + 1) * step], odd == 1)
        made_ref[1 - odd, n * step : (n + 1) * step] = own + sides_ref[there] + odd_beyond[there]
        made_ref[odd, n * step : (n + 1) * step] = odd_own[there] + beyond
        for column in range(2):
            into = out_any.at[there, column * WIDTH : (column + 1) * WIDTH]
            made = made_ref.at[column, n * step : (n + 1) * step]
            copies.append(pltpu.make_async_copy(made, into, sems.at[len(copies)]))
            copies[-1].start()
    for copy in copies:
        copy.wait()


def tied(value, *others):
    return lax.optimization_barrier((value, *others))[0]


def by_ring(relation, effects, phi_one, phi_two, innov_scale):
    gens, tms = lax.axis_size("gen"), lax.axis_size("tm")
    share = gens // tms
    half = gens // 2
    rows, depth = relation.shape
    cut = depth // 256 * 128
    wide = pl.cdiv(rows, 128) * 128
    long = rows + pl.cdiv(2 * wide // 128, 8) * 8
    order = list(range(0, gens, 2)) + list(range(gens - 1, 0, -2))
    forward = [(order[p], order[(p + 1) % gens]) for p in range(gens)]
    backward = [(b, a) for a, b in forward]
    swap = [(t, t ^ 1) for t in range(tms)]
    def spot_of():
        return Spot(gens, tms)

    def ahead_of(x):
        return lax.ppermute(x, "gen", backward)

    def behind_of(x):
        return lax.ppermute(x, "gen", forward)

    def multiplied(*fars, after=(), cost=1):
        parts = [tied(x, *after) for far in fars for x in blocks[far]]
        made = call(
            products_kernel,
            [(rows, WIDTH), (4, wide)] * len(fars),
            (relation, *parts),
            [pltpu.VMEM((rows, 2 * WIDTH), jnp.float32), pltpu.VMEM((wide, WIDTH), jnp.float32)],
            flops=cost * len(fars) * KERNEL_FLOPS,
        )
        for n, far in enumerate(fars):
            products[far] = made[2 * n : 2 * n + 2]

    def over_cores(x):
        return lax.ppermute(x, "tm", swap)

    def over_y(x):
        return lax.ppermute(x, "tm", [(t, t ^ 2) for t in range(tms)])

    def in_two_steps(behind, ahead, after=(), cost=1, between=lambda *made: None):
        both = pltpu.VMEM((rows, 2 * WIDTH), jnp.float32)
        parts = [tied(blocks[far][1], *after) for far in (behind, ahead)]
        bottoms = call(
            functools.partial(first_part_kernel, slice(cut, depth)),
            [(rows, WIDTH)] * 2,
            (relation, *parts),
            [both],
            flops=KERNEL_FLOPS,
        )
        between(*bottoms)
        made = call(
            functools.partial(last_part_kernel, slice(0, cut)),
            [(rows, WIDTH), (4, wide)] * 2,
            (relation, blocks[behind][0], blocks[ahead][0], *bottoms),
            [both, pltpu.VMEM((wide, WIDTH), jnp.float32)],
            flops=cost * KERNEL_FLOPS,
        )
        products[behind], products[ahead] = made[:2], made[2:]

    top, bottom = effects[:cut], effects[cut:]
    blocks, products = {0: (top, bottom)}, {}
    behind, ahead = blocks[0], blocks[0]
    multiplied(0)
    for n in range(1, half):
        behind_top = behind_of(behind[0] if n < 2 else tied(behind[0], *products[n - 2]))
        ahead_bottom = ahead_of(ahead[1])
        behind_bottom = behind_of(behind[1])
        ahead_top = ahead_of(ahead[0])
        behind, ahead = (behind_top, behind_bottom), (ahead_top, ahead_bottom)
        blocks[-n], blocks[n] = behind, ahead
        if n == 1:
            multiplied(-n, n)
        if n == 2:
            in_two_steps(-n, n, after=(), cost=1)
    two_send, two_keep = call(
        functools.partial(chip_pair_kernel, spot_of, 2),
        [(rows, WIDTH)] * 2,
        (products[2][0], products[-2][0]),
        flops=KERNEL_FLOPS // 2,
    )
    two_sum = call(sum_kernel, [(rows, WIDTH)], (two_keep, over_y(two_send)), flops=KERNEL_FLOPS // 10)[0]
    two_got = over_cores(two_sum)
    def last_step(*made):
        blocks[half] = (behind_of(tied(behind[0], *made)), ahead_of(ahead[1]))

    in_two_steps(1 - half, half - 1, cost=10, between=last_step)
    odd_fars = (-1, 3, 1, -3)
    send, keep = call(
        functools.partial(odd_kernel, spot_of, odd_fars),
        [(2 * long, WIDTH)] * 2,
        [tied(x, two_sum) for far in odd_fars for x in products[far]],
        [pltpu.VMEM((5, 4, wide), jnp.float32), pltpu.VMEM((2, long, WIDTH), jnp.float32)],
        flops=KERNEL_FLOPS // 2,
    )
    odd_send, odd_mine = call(
        functools.partial(part_sums_kernel, spot_of, odd_fars),
        [(long, WIDTH)] * 2,
        (keep, *[over_cores(send[i * (2 * long // 3) : (i + 1) * (2 * long // 3)]) for i in range(3)]),
        flops=KERNEL_FLOPS // 2,
    )
    odd_got = over_y(odd_send)
    both = pltpu.VMEM((rows, 2 * WIDTH), jnp.float32)
    top_product = call(
        functools.partial(first_part_kernel, slice(0, cut)),
        [(rows, WIDTH)],
        (relation, tied(blocks[half][0], odd_mine)),
        [both],
        flops=1 * KERNEL_FLOPS,
    )[0]
    products[half] = call(
        functools.partial(last_part_kernel, slice(cut, depth)),
        [(rows, WIDTH), (4, wide)],
        (relation, tied(blocks[half][1], odd_mine), top_product),
        [both, pltpu.VMEM((wide, WIDTH), jnp.float32)],
        flops=10 * KERNEL_FLOPS,
    )
    even_fars = (0, half, 2, -2)
    border_send, border_keep = call(
        functools.partial(borders_kernel, spot_of, even_fars),
        [(4, wide)] * 2,
        [products[far][1] for far in even_fars],
        [pltpu.VMEM((5, 4, wide), jnp.float32)],
        flops=KERNEL_FLOPS // 10,
    )
    border_send, border_mine = call(
        border_sums_kernel,
        [(2, wide)] * 2,
        (border_keep, over_cores(border_send)),
        flops=KERNEL_FLOPS // 10,
    )
    border_got = over_y(border_send)
    send_ours, send_theirs, keep = call(
        functools.partial(halves_kernel, spot_of, 0),
        [(rows // 2, WIDTH)] * 2 + [(rows, WIDTH)],
        [products[far][0] for far in (0, half)],
        flops=KERNEL_FLOPS // 2,
    )
    zero_send, zero_mine = call(
        half_sums_kernel,
        [(rows // 2, WIDTH)] * 2,
        (keep, over_cores(send_ours), over_cores(send_theirs)),
        flops=KERNEL_FLOPS // 10,
    )
    weights = call(weights_kernel, [(8, phi_one.shape[0])], (phi_one, phi_two, innov_scale))[0]
    odd_own, odd_beyond = call(
        functools.partial(odd_shares_kernel, spot_of),
        [(rows, WIDTH)] * 2,
        (odd_mine, odd_got, weights),
        [pltpu.VMEM((wide, WIDTH), jnp.float32)],
        flops=KERNEL_FLOPS,
    )
    zero_sum = call(
        sum_kernel,
        [(rows // 2, WIDTH)],
        (tied(zero_mine, border_got, odd_own), over_y(zero_send)),
        flops=KERNEL_FLOPS // 10,
    )[0]
    zero_got = over_cores(zero_sum)
    anywhere = pl.BlockSpec(memory_space=pl.ANY)
    given = (odd_own, odd_beyond, two_sum, two_got)
    scratch = [
        pltpu.VMEM((rows // 2, WIDTH), jnp.float32),
        pltpu.VMEM((2, rows // 2, WIDTH), jnp.float32),
        pltpu.SemaphoreType.DMA((10,)),
    ]
    applied, sides = call(
        functools.partial(last_kernel, spot_of, True),
        [(rows, share * WIDTH), (wide, WIDTH)],
        (*given, zero_sum, border_mine, border_got, weights),
        scratch,
        into=[anywhere, WHOLE],
    )
    return call(
        functools.partial(last_kernel, spot_of, False),
        [(rows, share * WIDTH)],
        (*given, zero_got, border_mine, border_got, weights, sides, applied),
        scratch,
        into=[anywhere],
        last=1,
    )[0]


def extended(cells, sides, width):
    for axis, dim in sides:
        count = lax.axis_size(axis)
        ends = count - 1
        head = lax.slice_in_dim(cells, 0, width, axis=dim)
        tail = lax.slice_in_dim(cells, cells.shape[dim] - width, cells.shape[dim], axis=dim)
        cells = jnp.concatenate(
            [
                lax.ppermute(tail, axis, [(i, (i + 1) % count) for i in range(ends)]),
                cells,
                lax.ppermute(head, axis, [((i + 1) % count, i) for i in range(ends)]),
            ],
            axis=dim,
        )
    return cells


def temporal_block(widened, first_time, phi_one, phi_two, innov_scale):
    block = widened.shape[1] - 4
    zero_pair = jnp.zeros((2,), jnp.float32)
    first_pad = jnp.concatenate([phi_one, zero_pair])
    second_pad = jnp.concatenate([phi_two, zero_pair])
    scale_pad = jnp.concatenate([innov_scale, zero_pair])
    first_win = lax.dynamic_slice_in_dim(first_pad, first_time, block + 2)
    second_win = lax.dynamic_slice_in_dim(second_pad, first_time, block + 2)
    scale_win = lax.dynamic_slice_in_dim(scale_pad, first_time, block + 2)
    innov = (
        widened[:, 2:]
        - first_win[None, :] * widened[:, 1:-1]
        - second_win[None, :] * widened[:, :-2]
    )
    weighted = scale_win[None, :] * innov
    first_next = lax.dynamic_slice_in_dim(first_pad, first_time + 1, block)
    second_next = lax.dynamic_slice_in_dim(second_pad, first_time + 2, block)
    return (
        weighted[:, :block]
        - first_next[None, :] * weighted[:, 1 : block + 1]
        - second_next[None, :] * weighted[:, 2 : block + 2]
    )


def by_gather(relation, effects, phi_one, phi_two, innov_scale):
    relation_wide = relation.astype(jnp.float32)
    partial_sums = jnp.dot(
        relation_wide,
        lax.all_gather(effects, "gen", axis=1, tiled=True),
        precision=lax.Precision.HIGHEST,
        preferred_element_type=jnp.float32,
    )
    genetic = lax.psum_scatter(partial_sums, "tm", scatter_dimension=1, tiled=True)
    widened_time = extended(genetic, (("tm", 1),), 2)
    start_tm = lax.axis_index("tm") * genetic.shape[1]
    return temporal_block(widened_time, start_tm, phi_one, phi_two, innov_scale)


def on_device(relation, effects, phi_one, phi_two, innov_scale):
    gens, tms = lax.axis_size("gen"), lax.axis_size("tm")
    fits = gens == 8 and tms == 4 and effects.shape[1] == WIDTH and effects.shape[0] % 64 == 0 and relation.shape[0] % 160 == 0
    way = by_ring if fits else by_gather
    return way(relation, effects, phi_one, phi_two, innov_scale)


def solution(mesh):
    placed = (P("gen", "tm"), P("tm", "gen"), P(), P(), P())
    return jax.shard_map(
        on_device, mesh=mesh, in_specs=placed, out_specs=P("gen", "tm"), check_vma=False
    )
```

```python
import functools

import jax
import jax.numpy as jnp
from jax import lax
from jax.experimental import pallas as pl
from jax.experimental.pallas import tpu as pltpu
from jax.sharding import PartitionSpec as P

VMEM_LIMIT = 12 * 1024 * 1024
WIDTH = 128
KERNEL_FLOPS = 10**8

WHOLE = pl.BlockSpec(memory_space=pltpu.VMEM)


def call(kernel, shapes, operands, scratch=(), flops=0, into=None, last=0):
    return pl.pallas_call(
        kernel,
        out_shape=[jax.ShapeDtypeStruct(shape, jnp.float32) for shape in shapes],
        in_specs=[WHOLE] * (len(operands) - last) + (into[:last] if last else []),
        input_output_aliases={len(operands) - last + n: n for n in range(last)},
        out_specs=into or [WHOLE] * len(shapes),
        scratch_shapes=scratch,
        compiler_params=pltpu.CompilerParams(vmem_limit_bytes=VMEM_LIMIT),
        cost_estimate=pl.CostEstimate(flops=flops, bytes_accessed=0, transcendentals=0),
    )(*operands)


def bands(phi_one, phi_two, innov_scale):
    count = phi_one.shape[1]
    row = lax.broadcasted_iota(jnp.int32, (8, count), 0)
    lane = lax.broadcasted_iota(jnp.int32, (8, count), 1)

    def rows(*values):
        out = jnp.zeros((8, count), jnp.float32)
        for n, value in enumerate(values):
            out = jnp.where(row == n, value, out)
        return out

    now = rows(phi_one, phi_two, innov_scale)
    next_1 = jnp.where(lane < count - 1, pltpu.roll(now, count - 1, 1), 0.0)
    next_2 = jnp.where(lane < count - 2, pltpu.roll(now, count - 2, 1), 0.0)
    first_0, second_0, scale_0 = (now[n : n + 1] for n in range(3))
    first_1, second_1, scale_1 = (next_1[n : n + 1] for n in range(3))
    first_2, second_2, scale_2 = (next_2[n : n + 1] for n in range(3))
    return rows(
        -scale_0 * second_0,
        first_1 * scale_1 * second_1 - scale_0 * first_0,
        scale_0 + first_1 * first_1 * scale_1 + second_2 * second_2 * scale_2,
        second_2 * scale_2 * first_2 - first_1 * scale_1,
        -second_2 * scale_2,
    )


class Spot:
    def __init__(self, gens, tms):
        self.gens, self.share, self.half = gens, gens // tms, gens // 2
        self.gen, self.tm = lax.axis_index("gen"), lax.axis_index("tm")
        self.place = self.place_of(self.gen)

    def place_of(self, gen):
        return jnp.where(gen % 2 == 0, gen // 2, self.gens - 1 - gen // 2)

    def block_at(self, far):
        p = (self.place + (far + self.gens)) % self.gens
        return jnp.where(p < self.half, 2 * p, 2 * (self.gens - 1 - p) + 1)

    def owner_of(self, far):
        return self.block_at(far) // self.share

    def keeps(self, far):
        return jnp.where(self.owner_of(far) % 2 == self.tm % 2, 1, 0)

    def border_of(self, far, fars):
        there = (2 * self.gens - 2 * self.place - far) % self.gens
        at = jnp.int32(len(fars))
        for m, other in enumerate(fars):
            if other != far:
                at = jnp.where(there == other % self.gens, m, at)
        return at


def weights_kernel(one_ref, two_ref, scale_ref, weights_ref):
    weights_ref[...] = bands(one_ref[...][None], two_ref[...][None], scale_ref[...][None])


def products_kernel(relation_ref, *refs):
    both_ref, padded_ref = refs[-2:]
    count = (len(refs) - 2) // 4
    rows = relation_ref.shape[0]
    padded_ref[...] = jnp.zeros_like(padded_ref)
    for n in range(count):
        block = jnp.concatenate([refs[2 * n][...], refs[2 * n + 1][...]], axis=0)
        high = block.astype(jnp.bfloat16)
        low = (block - high.astype(jnp.float32)).astype(jnp.bfloat16)
        both_ref[...] = jnp.dot(
            relation_ref[...],
            jnp.concatenate([high, low], axis=1),
            preferred_element_type=jnp.float32,
        )
        padded_ref[:rows] = both_ref[:, :WIDTH] + both_ref[:, WIDTH:]
        refs[2 * count + 2 * n][...] = padded_ref[:rows]
        turned = padded_ref[...].T
        edges_ref = refs[2 * count + 2 * n + 1]
        edges_ref[0:2] = turned[0:2]
        edges_ref[2:4] = turned[WIDTH - 2 :]


def first_part_kernel(columns, relation_ref, *refs):
    both_ref = refs[-1]
    count = (len(refs) - 1) // 2
    for n in range(count):
        both_ref[...] = jnp.dot(
            relation_ref[:, columns], two_parts(refs[n][...]), preferred_element_type=jnp.float32
        )
        refs[count + n][...] = both_ref[:, :WIDTH] + both_ref[:, WIDTH:]


def last_part_kernel(columns, relation_ref, *refs):
    both_ref, padded_ref = refs[-2:]
    count = (len(refs) - 2) // 4
    rows = relation_ref.shape[0]
    padded_ref[...] = jnp.zeros_like(padded_ref)
    for n in range(count):
        both_ref[...] = jnp.dot(
            relation_ref[:, columns], two_parts(refs[n][...]), preferred_element_type=jnp.float32
        )
        padded_ref[:rows] = both_ref[:, :WIDTH] + both_ref[:, WIDTH:] + refs[count + n][...]
        refs[2 * count + 2 * n][...] = padded_ref[:rows]
        turned = padded_ref[...].T
        edges_ref = refs[2 * count + 2 * n + 1]
        edges_ref[0:2] = turned[0:2]
        edges_ref[2:4] = turned[WIDTH - 2 :]


def two_parts(block):
    high = block.astype(jnp.bfloat16)
    low = (block - high.astype(jnp.float32)).astype(jnp.bfloat16)
    return jnp.concatenate([high, low], axis=1)


def odd_kernel(spot_of, fars, *refs):
    send_ref, keep_ref, edges_ref, message_ref = refs[-4:]
    spot = spot_of()
    rows, long = refs[0].shape[0], message_ref.shape[1]
    for m in range(4):
        edges_ref[m] = refs[2 * m + 1][...]
    edges_ref[4] = jnp.zeros_like(refs[1])
    for m in range(4):
        there = edges_ref[spot.border_of(fars[m], fars)]
        border = jnp.where(spot.block_at(fars[m]) % spot.share == 0, there[2:4], there[0:2])
        message_ref[m % 2, :rows] = refs[2 * m][...]
        message_ref[m % 2, rows:] = jnp.zeros((long - rows, WIDTH), jnp.float32)
        for k in range(border.shape[1] // WIDTH):
            message_ref[m % 2, rows + 2 * k : rows + 2 * k + 2] = border[:, k * WIDTH : (k + 1) * WIDTH]
        if m % 2:
            here = pl.ds(m // 2 * long, long)
            near = spot.keeps(fars[m - 1])
            keep_ref[here] = message_ref[1 - near]
            send_ref[here] = message_ref[near]


def halves_kernel(spot_of, near, near_ref, far_ref, send_ours, send_theirs, keep_ref):
    spot = spot_of()
    rows = near_ref.shape[0] // 2
    core = spot.tm % 2
    mine = spot.owner_of(near) // 2 == spot.tm // 2
    for ours in (True, False):

        @pl.when(mine == ours)
        def _():
            pairs = ((near_ref, send_ours), (far_ref, send_theirs))
            if not ours:
                pairs = ((far_ref, send_ours), (near_ref, send_theirs))
            for n, (ref, send_ref) in enumerate(pairs):
                send_ref[...] = ref[pl.ds(pl.multiple_of((1 - core) * rows, 8), rows)]
                keep_ref[pl.ds(n * rows, rows)] = ref[pl.ds(pl.multiple_of(core * rows, 8), rows)]


def half_sums_kernel(keep_ref, got_ours, got_theirs, send_ref, mine_ref):
    rows = mine_ref.shape[0]
    mine_ref[...] = keep_ref[:rows] + got_ours[...]
    send_ref[...] = keep_ref[rows:] + got_theirs[...]


def chip_pair_kernel(spot_of, near, near_ref, far_ref, send_ref, keep_ref):
    spot = spot_of()
    mine = spot.owner_of(near) // 2 == spot.tm // 2

    @pl.when(mine)
    def _():
        keep_ref[...] = near_ref[...]
        send_ref[...] = far_ref[...]

    @pl.when(jnp.logical_not(mine))
    def _():
        keep_ref[...] = far_ref[...]
        send_ref[...] = near_ref[...]


def borders_kernel(spot_of, fars, *refs):
    send_ref, keep_ref, edges_ref = refs[-3:]
    spot = spot_of()
    for m in range(4):
        edges_ref[m] = refs[m][...]
    edges_ref[4] = jnp.zeros_like(refs[0])
    chip, core = spot.tm // 2, spot.tm % 2
    send_ref[...] = jnp.zeros_like(send_ref)
    keep_ref[...] = jnp.zeros_like(keep_ref)
    for m, far in enumerate(fars):
        owner = spot.owner_of(far)
        there = edges_ref[spot.border_of(far, fars)]
        border = jnp.where(spot.block_at(far) % spot.share == 0, there[2:4], there[0:2])
        for n in range(2):
            for out_ref, whose in ((send_ref, 1 - core), (keep_ref, core)):
                wanted = 2 * jnp.where(n == 0, chip, 1 - chip) + whose

                @pl.when(owner == wanted)
                def _():
                    out_ref[2 * n : 2 * n + 2] = border


def border_sums_kernel(keep_ref, got_ref, send_ref, mine_ref):
    mine_ref[...] = keep_ref[0:2] + got_ref[0:2]
    send_ref[...] = keep_ref[2:4] + got_ref[2:4]


def sum_kernel(one_ref, other_ref, out_ref):
    out_ref[...] = one_ref[...] + other_ref[...]


def part_sums_kernel(spot_of, fars, keep_ref, *refs):
    spot = spot_of()
    owner = jnp.where(spot.keeps(fars[0]) == 1, spot.owner_of(fars[0]), spot.owner_of(fars[1]))
    mine = jnp.where(owner // 2 == spot.tm // 2, 0, 1)
    rows = refs[-1].shape[0]
    for n in range(2):

        @pl.when(mine == n)
        def _():
            here, there = slice(n * rows, (n + 1) * rows), slice((1 - n) * rows, (2 - n) * rows)
            size = refs[0].shape[0]
            for out_ref, block in ((refs[-2], there), (refs[-1], here)):
                for m, got_ref in enumerate(refs[:-2]):
                    first, end = max(block.start, m * size), min(block.stop, (m + 1) * size)
                    if first < end:
                        out_ref[first - block.start : end - block.start] = (
                            keep_ref[first:end] + got_ref[first - m * size : end - m * size]
                        )


def row_weights(weights, far, lanes):
    return jnp.where(lanes, weights[2 + far : 3 + far], 0.0)


def beside(weights, border, left):
    span = border.shape[1]
    row = lax.broadcasted_iota(jnp.int32, (8, span), 0)
    nothing = jnp.zeros((WIDTH - 8, span), jnp.float32)
    end = WIDTH - 1
    first = weights[0:1, 0:1] * border[0:1] + weights[1:2, 0:1] * border[1:2]
    second = weights[0:1, 1:2] * border[1:2]
    above = jnp.where(row == 0, first, jnp.where(row == 1, second, 0.0))
    last = weights[3:4, end:] * border[0:1] + weights[4:5, end:] * border[1:2]
    but_last = weights[4:5, end - 1 : end] * border[0:1]
    below = jnp.where(row == 7, last, jnp.where(row == 6, but_last, 0.0))
    none = jnp.zeros_like(above)
    return jnp.concatenate(
        [jnp.where(left, above, none), nothing[: WIDTH - 16], jnp.where(left, none, below)], axis=0
    ).T


def shares(weights, other_weights, block, left):
    lane = lax.broadcasted_iota(jnp.int32, (1, WIDTH), 1)
    own = weights[2:3] * block
    beyond = 0.0
    for far in (1, 2):
        back, on = pltpu.roll(block, far, 1), pltpu.roll(block, WIDTH - far, 1)
        own += row_weights(weights, -far, lane >= far) * back
        own += row_weights(weights, far, lane < WIDTH - far) * on
        beyond += jnp.where(
            left,
            row_weights(other_weights, -far, lane < far) * back,
            row_weights(other_weights, far, lane >= WIDTH - far) * on,
        )
    return own, beyond


def odd_column(spot):
    return jnp.where((spot.place_of(spot.share * spot.tm) + spot.place) % 2 == 0, 1, 0)


def column_weights(spot, weights_ref, column):
    start = (spot.tm * 2 + column) * WIDTH
    return weights_ref[:, pl.ds(pl.multiple_of(start, WIDTH), WIDTH)]


def odd_shares_kernel(spot_of, mine_ref, got_ref, weights_ref, own_ref, beyond_ref, sides_ref):
    spot = spot_of()
    odd = odd_column(spot)
    rows, span = own_ref.shape[0], sides_ref.shape[0]
    weights = column_weights(spot, weights_ref, odd)
    others = column_weights(spot, weights_ref, 1 - odd)
    extra = mine_ref[rows:] + got_ref[rows:]
    border = jnp.concatenate([extra[2 * k : 2 * k + 2] for k in range(span // WIDTH)], axis=1)
    sides_ref[...] = beside(weights, border, odd == 0)
    step = rows // 5
    for n in range(5):
        here = slice(n * step, (n + 1) * step)
        own, beyond = shares(weights, others, mine_ref[here] + got_ref[here], odd == 0)
        own_ref[here] = own + sides_ref[here]
        beyond_ref[here] = beyond


def last_kernel(
    spot_of,
    same,
    odd_own,
    odd_beyond,
    two_sum,
    two_got,
    zero_half,
    border_mine,
    border_got,
    weights_ref,
    *refs,
):
    out_any, sides_ref, even_ref, made_ref, sems = refs[-5:] if same else (refs[-4], refs[0], *refs[-3:])
    spot = spot_of()
    odd = odd_column(spot)
    rows = out_any.shape[0] // 2
    core = spot.tm % 2
    first = pl.multiple_of((core if same else 1 - core) * rows, 8)
    here = pl.ds(first, rows)
    is_two = (spot.owner_of(2) == spot.tm) | (spot.owner_of(-2) == spot.tm)

    @pl.when(is_two)
    def _():
        even_ref[...] = two_sum[here] + two_got[here]

    @pl.when(jnp.logical_not(is_two))
    def _():
        even_ref[...] = zero_half[...]

    weights = column_weights(spot, weights_ref, 1 - odd)
    others = column_weights(spot, weights_ref, odd)
    if same:
        sides_ref[...] = beside(weights, border_mine[...] + border_got[...], odd == 1)
    pieces = 2
    step = rows // pieces
    copies = []
    for n in range(pieces):
        there = pl.ds(pl.multiple_of(first + n * step, 8), step)
        own, beyond = shares(weights, others, even_ref[n * step : (n + 1) * step], odd == 1)
        made_ref[1 - odd, n * step : (n + 1) * step] = own + sides_ref[there] + odd_beyond[there]
        made_ref[odd, n * step : (n + 1) * step] = odd_own[there] + beyond
        for column in range(2):
            into = out_any.at[there, column * WIDTH : (column + 1) * WIDTH]
            made = made_ref.at[column, n * step : (n + 1) * step]
            copies.append(pltpu.make_async_copy(made, into, sems.at[len(copies)]))
            copies[-1].start()
    for copy in copies:
        copy.wait()


def tied(value, *others):
    return lax.optimization_barrier((value, *others))[0]


def by_ring(relation, effects, phi_one, phi_two, innov_scale):
    gens, tms = lax.axis_size("gen"), lax.axis_size("tm")
    share = gens // tms
    half = gens // 2
    rows, depth = relation.shape
    cut = depth // 256 * 128
    wide = pl.cdiv(rows, 128) * 128
    long = rows + pl.cdiv(2 * wide // 128, 8) * 8
    order = list(range(0, gens, 2)) + list(range(gens - 1, 0, -2))
    forward = [(order[p], order[(p + 1) % gens]) for p in range(gens)]
    backward = [(b, a) for a, b in forward]
    swap = [(t, t ^ 1) for t in range(tms)]
    def spot_of():
        return Spot(gens, tms)

    def ahead_of(x):
        return lax.ppermute(x, "gen", backward)

    def behind_of(x):
        return lax.ppermute(x, "gen", forward)

    def multiplied(*fars, after=(), cost=1):
        parts = [tied(x, *after) for far in fars for x in blocks[far]]
        made = call(
            products_kernel,
            [(rows, WIDTH), (4, wide)] * len(fars),
            (relation, *parts),
            [pltpu.VMEM((rows, 2 * WIDTH), jnp.float32), pltpu.VMEM((wide, WIDTH), jnp.float32)],
            flops=cost * len(fars) * KERNEL_FLOPS,
        )
        for n, far in enumerate(fars):
            products[far] = made[2 * n : 2 * n + 2]

    def over_cores(x):
        return lax.ppermute(x, "tm", swap)

    def over_y(x):
        return lax.ppermute(x, "tm", [(t, t ^ 2) for t in range(tms)])

    def in_two_steps(behind, ahead, after=(), cost=1, between=lambda *made: None):
        both = pltpu.VMEM((rows, 2 * WIDTH), jnp.float32)
        parts = [tied(blocks[far][1], *after) for far in (behind, ahead)]
        bottoms = call(
            functools.partial(first_part_kernel, slice(cut, depth)),
            [(rows, WIDTH)] * 2,
            (relation, *parts),
            [both],
            flops=KERNEL_FLOPS,
        )
        between(*bottoms)
        made = call(
            functools.partial(last_part_kernel, slice(0, cut)),
            [(rows, WIDTH), (4, wide)] * 2,
            (relation, blocks[behind][0], blocks[ahead][0], *bottoms),
            [both, pltpu.VMEM((wide, WIDTH), jnp.float32)],
            flops=cost * KERNEL_FLOPS,
        )
        products[behind], products[ahead] = made[:2], made[2:]

    top, bottom = effects[:cut], effects[cut:]
    blocks, products = {0: (top, bottom)}, {}
    behind, ahead = blocks[0], blocks[0]
    multiplied(0)
    for n in range(1, half):
        behind_top = behind_of(behind[0] if n < 2 else tied(behind[0], *products[n - 2]))
        ahead_bottom = ahead_of(ahead[1])
        behind_bottom = behind_of(behind[1])
        ahead_top = ahead_of(ahead[0])
        behind, ahead = (behind_top, behind_bottom), (ahead_top, ahead_bottom)
        blocks[-n], blocks[n] = behind, ahead
        if n == 1:
            multiplied(-n, n)
        if n == 2:
            in_two_steps(-n, n, after=(), cost=1)
    two_send, two_keep = call(
        functools.partial(chip_pair_kernel, spot_of, 2),
        [(rows, WIDTH)] * 2,
        (products[2][0], products[-2][0]),
        flops=KERNEL_FLOPS // 2,
    )
    two_sum = call(sum_kernel, [(rows, WIDTH)], (two_keep, over_y(two_send)), flops=KERNEL_FLOPS // 10)[0]
    two_got = over_cores(two_sum)
    def last_step(*made):
        blocks[half] = (behind_of(tied(behind[0], *made)), ahead_of(tied(ahead[1], *made)))

    in_two_steps(1 - half, half - 1, cost=10, between=last_step)
    odd_fars = (-1, 3, 1, -3)
    send, keep = call(
        functools.partial(odd_kernel, spot_of, odd_fars),
        [(2 * long, WIDTH)] * 2,
        [tied(x, two_sum) for far in odd_fars for x in products[far]],
        [pltpu.VMEM((5, 4, wide), jnp.float32), pltpu.VMEM((2, long, WIDTH), jnp.float32)],
        flops=KERNEL_FLOPS // 2,
    )
    odd_send, odd_mine = call(
        functools.partial(part_sums_kernel, spot_of, odd_fars),
        [(long, WIDTH)] * 2,
        (keep, *[over_cores(send[i * (2 * long // 3) : (i + 1) * (2 * long // 3)]) for i in range(3)]),
        flops=KERNEL_FLOPS // 2,
    )
    odd_got = over_y(odd_send)
    both = pltpu.VMEM((rows, 2 * WIDTH), jnp.float32)
    top_product = call(
        functools.partial(first_part_kernel, slice(0, cut)),
        [(rows, WIDTH)],
        (relation, tied(blocks[half][0], odd_mine)),
        [both],
        flops=1 * KERNEL_FLOPS,
    )[0]
    products[half] = call(
        functools.partial(last_part_kernel, slice(cut, depth)),
        [(rows, WIDTH), (4, wide)],
        (relation, tied(blocks[half][1], odd_mine), top_product),
        [both, pltpu.VMEM((wide, WIDTH), jnp.float32)],
        flops=10 * KERNEL_FLOPS,
    )
    even_fars = (0, half, 2, -2)
    border_send, border_keep = call(
        functools.partial(borders_kernel, spot_of, even_fars),
        [(4, wide)] * 2,
        [products[far][1] for far in even_fars],
        [pltpu.VMEM((5, 4, wide), jnp.float32)],
        flops=KERNEL_FLOPS // 10,
    )
    border_send, border_mine = call(
        border_sums_kernel,
        [(2, wide)] * 2,
        (border_keep, over_cores(border_send)),
        flops=KERNEL_FLOPS // 10,
    )
    border_got = over_y(border_send)
    send_ours, send_theirs, keep = call(
        functools.partial(halves_kernel, spot_of, 0),
        [(rows // 2, WIDTH)] * 2 + [(rows, WIDTH)],
        [products[far][0] for far in (0, half)],
        flops=KERNEL_FLOPS // 2,
    )
    zero_send, zero_mine = call(
        half_sums_kernel,
        [(rows // 2, WIDTH)] * 2,
        (keep, over_cores(send_ours), over_cores(send_theirs)),
        flops=KERNEL_FLOPS // 10,
    )
    weights = call(weights_kernel, [(8, phi_one.shape[0])], (phi_one, phi_two, innov_scale))[0]
    odd_own, odd_beyond = call(
        functools.partial(odd_shares_kernel, spot_of),
        [(rows, WIDTH)] * 2,
        (odd_mine, odd_got, weights),
        [pltpu.VMEM((wide, WIDTH), jnp.float32)],
        flops=KERNEL_FLOPS,
    )
    zero_sum = call(
        sum_kernel,
        [(rows // 2, WIDTH)],
        (tied(zero_mine, border_got, odd_own), over_y(zero_send)),
        flops=KERNEL_FLOPS // 10,
    )[0]
    zero_got = over_cores(zero_sum)
    anywhere = pl.BlockSpec(memory_space=pl.ANY)
    given = (odd_own, odd_beyond, two_sum, two_got)
    scratch = [
        pltpu.VMEM((rows // 2, WIDTH), jnp.float32),
        pltpu.VMEM((2, rows // 2, WIDTH), jnp.float32),
        pltpu.SemaphoreType.DMA((4,)),
    ]
    applied, sides = call(
        functools.partial(last_kernel, spot_of, True),
        [(rows, share * WIDTH), (wide, WIDTH)],
        (*given, zero_sum, border_mine, border_got, weights),
        scratch,
        into=[anywhere, WHOLE],
    )
    return call(
        functools.partial(last_kernel, spot_of, False),
        [(rows, share * WIDTH)],
        (*given, zero_got, border_mine, border_got, weights, sides, applied),
        scratch,
        into=[anywhere],
        last=1,
    )[0]


def extended(cells, sides, width):
    for axis, dim in sides:
        count = lax.axis_size(axis)
        ends = count - 1
        head = lax.slice_in_dim(cells, 0, width, axis=dim)
        tail = lax.slice_in_dim(cells, cells.shape[dim] - width, cells.shape[dim], axis=dim)
        cells = jnp.concatenate(
            [
                lax.ppermute(tail, axis, [(i, (i + 1) % count) for i in range(ends)]),
                cells,
                lax.ppermute(head, axis, [((i + 1) % count, i) for i in range(ends)]),
            ],
            axis=dim,
        )
    return cells


def temporal_block(widened, first_time, phi_one, phi_two, innov_scale):
    block = widened.shape[1] - 4
    zero_pair = jnp.zeros((2,), jnp.float32)
    first_pad = jnp.concatenate([phi_one, zero_pair])
    second_pad = jnp.concatenate([phi_two, zero_pair])
    scale_pad = jnp.concatenate([innov_scale, zero_pair])
    first_win = lax.dynamic_slice_in_dim(first_pad, first_time, block + 2)
    second_win = lax.dynamic_slice_in_dim(second_pad, first_time, block + 2)
    scale_win = lax.dynamic_slice_in_dim(scale_pad, first_time, block + 2)
    innov = (
        widened[:, 2:]
        - first_win[None, :] * widened[:, 1:-1]
        - second_win[None, :] * widened[:, :-2]
    )
    weighted = scale_win[None, :] * innov
    first_next = lax.dynamic_slice_in_dim(first_pad, first_time + 1, block)
    second_next = lax.dynamic_slice_in_dim(second_pad, first_time + 2, block)
    return (
        weighted[:, :block]
        - first_next[None, :] * weighted[:, 1 : block + 1]
        - second_next[None, :] * weighted[:, 2 : block + 2]
    )


def by_gather(relation, effects, phi_one, phi_two, innov_scale):
    relation_wide = relation.astype(jnp.float32)
    partial_sums = jnp.dot(
        relation_wide,
        lax.all_gather(effects, "gen", axis=1, tiled=True),
        precision=lax.Precision.HIGHEST,
        preferred_element_type=jnp.float32,
    )
    genetic = lax.psum_scatter(partial_sums, "tm", scatter_dimension=1, tiled=True)
    widened_time = extended(genetic, (("tm", 1),), 2)
    start_tm = lax.axis_index("tm") * genetic.shape[1]
    return temporal_block(widened_time, start_tm, phi_one, phi_two, innov_scale)


def on_device(relation, effects, phi_one, phi_two, innov_scale):
    gens, tms = lax.axis_size("gen"), lax.axis_size("tm")
    fits = gens == 8 and tms == 4 and effects.shape[1] == WIDTH and effects.shape[0] % 64 == 0 and relation.shape[0] % 160 == 0
    way = by_ring if fits else by_gather
    return way(relation, effects, phi_one, phi_two, innov_scale)


def solution(mesh):
    placed = (P("gen", "tm"), P("tm", "gen"), P(), P(), P())
    return jax.shard_map(
        on_device, mesh=mesh, in_specs=placed, out_specs=P("gen", "tm"), check_vma=False
    )
```
